128 devices in a mesh: dev: 128 (over z, y, x, core).
Axes of the slice: x: 4, y: 4, z: 4, core: 2. Of those that a mesh axis runs over, the one named last changes fastest.
Arguments:
- pose_input: bfloat16 [16384, 256], P('dev'), may hold values from -6 to 6
- w_in: bfloat16 [256, 1024], replicated, may hold values from -0.375 to 0.375
- w_hid: bfloat16 [1024, 1024], replicated, may hold values from -0.1875 to 0.1875
- w_out: bfloat16 [1024, 256], replicated, may hold values from -0.1875 to 0.1875
- targets: bfloat16 [16384, 15744], P('dev'), may hold values from -6 to 6
- basis: bfloat16 [128, 256, 15744], P('dev'), may hold values from -0.375 to 0.375
- owner: int32 [128], replicated, may hold values from 0 to 127, each once
- frame_subject: int32 [16384, 1], P('dev'), may hold values from 0 to 127; in each aligned block of 128 rows (0 to 127, 128 to 255, ...) at most 2 rows name the same one
Outputs:
- grad_w_in: float32 [256, 1024], P(None, 'dev')
- grad_w_hid: float32 [1024, 1024], P('dev')
- grad_w_out: float32 [1024, 256], P('dev')
- grad_basis: bfloat16 [128, 256, 15744], P('dev')
The draws below stay inside these ranges and needn't reach their ends.
Inputs may be any that keep to these rules, and one draw needn't show every extreme that they name: owner is a permutation: each slot holds exactly one subject. `frame_subject`: among the 128 frames of one device no subject appears more than 2 times.
All inputs are finite; a program needn't handle non-finite values.
Results may differ from the reference program's by a relative error of at most 0.0063.
Values may be sent and summed in bfloat16 or wider, within the bound.
A program may use at most 128 MiB of HBM per device.

```python
import math
import jax
import jax.numpy as jnp
import numpy as np
from jax import lax

P_SIZE = 256
V3 = 15744
H = 1024
FR_DEV = 128
CAP = 2
SUBJECTS = 128
FRAMES = 16384
N_DEV = 128


def levels(own_key, dims, cuts, smallest, largest):
    factor_of, own = 1.0, jax.random.fold_in(own_key, 6)
    for dim, parts in cuts:
        steps = jnp.exp(jax.random.uniform(jax.random.fold_in(own, dim), (parts,), jnp.float32, smallest / len(cuts), largest / len(cuts)))
        factor_of = factor_of * jnp.repeat(steps, dims[dim] // parts).reshape([-1 if axis == dim else 1 for axis in range(len(dims))])
    return factor_of


def assign_block(rng, own, number, rows, amount, top, bound, lean):
    sequence = jax.random.permutation(rng, amount)
    crowded, ordinary = portions_of(amount, rows * top, bound, lean, True), portions_of(amount, rows * top, bound, lean, False)
    places = jnp.arange(amount)

    def named(lengths, rotation):
        used = int((lengths > 0).sum())
        fixed = max(1, used // 4)
        moved = fixed + (places - fixed + rotation * (used - fixed)) % max(1, amount - fixed)
        return jnp.zeros((amount,), jnp.int32).at[sequence[jnp.where(places < fixed, places, moved)]].set(jnp.asarray(lengths, jnp.int32))

    lengths = jnp.where(number % 4 == 0, named(crowded, number // 4), named(ordinary, number - number // 4 - 1))
    mixed = jax.random.permutation(jax.random.fold_in(own, 3), amount)
    source_of, sink = mixed[0:amount // 2 * 2:2], mixed[1:amount // 2 * 2:2]
    margin = jnp.minimum(lengths[source_of] - 1, bound - lengths[sink]) // 2
    margin = jnp.where((source_of == sequence[0]) | (sink == sequence[0]) | (lengths[sink] == 0), 0, jnp.maximum(margin, 0))
    moved = jax.random.randint(jax.random.fold_in(own, 4), (amount // 2,), 0, 1 << 20) % (margin + 1)
    lengths = lengths.at[source_of].add(-moved).at[sink].add(moved)
    members = jnp.searchsorted(jnp.cumsum(lengths), jnp.arange(rows * top), side="right").astype(jnp.int32)
    table = members.reshape(top, rows).T
    table = table[jax.random.permutation(jax.random.fold_in(own, 1), rows)]
    rotation = jax.random.randint(jax.random.fold_in(own, 2), (rows, 1), 0, top)
    return jnp.take_along_axis(table, (jnp.arange(top)[None, :] + rotation) % top, axis=1)


def portions_of(count, total, bound, skew, full):
    weights = [(1 << 20) // math.isqrt(rank ** skew) + 1 for rank in range(1, count + 1)]
    largest = bound if full else min(bound, max(-(-total // count), total * weights[0] // sum(weights)))
    least = 1 if total - largest >= count - 1 else 0
    given, rest = [largest] + [least] * (count - 1), total - largest - least * (count - 1)
    while rest > 0:
        candidates = [i for i in range(1, count) if given[i] < largest] or [i for i in range(1, count) if given[i] < bound]
        mass, budget = sum([weights[i] for i in candidates]), rest
        for i in candidates:
            extra = min(bound - given[i], max(1, budget * weights[i] // mass), rest)
            given[i] = given[i] + extra
            rest = rest - extra
    return np.array(given)


def scatter_about(key, shape, deviation, reach, split=(), kind=jnp.bfloat16):
    entries = deviation * jax.random.normal(key, shape, jnp.float32)
    if split:
        entries = entries * levels(key, shape, split, -0.22, 0.18)
    return jnp.clip(entries, -reach, reach).astype(kind)


def setup_inputs(seed: int = 0) -> dict:
    arg_keys = jax.random.split(jax.random.key(seed), 9)
    pose_input = scatter_about(arg_keys[0], (FRAMES, P_SIZE), 1.0, 6.0, ((0, 128),))
    w_in = scatter_about(arg_keys[1], (P_SIZE, H), P_SIZE ** -0.5, 0.375)
    w_hid = scatter_about(arg_keys[2], (H, H), H ** -0.5, 0.1875)
    w_out = scatter_about(arg_keys[3], (H, P_SIZE), H ** -0.5, 0.1875)
    targets = scatter_about(arg_keys[4], (FRAMES, V3), 1.0, 6.0, ((0, 128),))
    basis = scatter_about(arg_keys[5], (N_DEV, P_SIZE, V3), P_SIZE ** -0.5, 0.375, ((0, 128),))
    owner = jax.random.permutation(arg_keys[6], SUBJECTS).astype(jnp.int32)
    frame_subject_keys = jax.random.split(jax.random.fold_in(arg_keys[7], 1), FRAMES // FR_DEV)
    frame_subject_turns = jax.random.permutation(jax.random.fold_in(arg_keys[7], 3), FRAMES // FR_DEV)
    frame_subject = jax.vmap(lambda own, number: assign_block(jax.random.fold_in(arg_keys[7], 2), own, number, FR_DEV, SUBJECTS, 1, CAP, 2))(frame_subject_keys, frame_subject_turns).reshape((FRAMES, 1))
    return {"pose_input": pose_input, "w_in": w_in, "w_hid": w_hid, "w_out": w_out, "targets": targets, "basis": basis, "owner": owner, "frame_subject": frame_subject}


def silu_slope(value):
    sig = jax.nn.sigmoid(value)
    return sig * (1.0 + value * (1.0 - sig))


def reference(pose_input, w_in, w_hid, w_out, targets, basis, owner, frame_subject):
    pre_one = jnp.dot(pose_input, w_in, preferred_element_type=jnp.float32)
    hidden_one = jax.nn.silu(pre_one).astype(jnp.bfloat16)
    pre_two = jnp.dot(hidden_one, w_hid, preferred_element_type=jnp.float32)
    hidden_two = jax.nn.silu(pre_two).astype(jnp.bfloat16)
    features = jnp.dot(hidden_two, w_out, preferred_element_type=jnp.float32).astype(jnp.bfloat16)
    subject = frame_subject[:, 0].astype(jnp.int32)
    dest_slot = owner[subject].astype(jnp.int32)
    order = jnp.argsort(dest_slot, stable=True).astype(jnp.int32)
    slots = jnp.arange(N_DEV, dtype=jnp.int32)
    counts = jnp.sum((dest_slot[:, None] == slots[None, :]).astype(jnp.int32), axis=0)
    offsets = (jnp.cumsum(counts) - counts).astype(jnp.int32)
    window = N_DEV * CAP
    order_padded = jnp.concatenate([order, jnp.zeros((window,), jnp.int32)])
    scale = V3 ** -0.5

    def per_slot(item):
        slot, slot_basis = item
        rows = lax.dynamic_slice_in_dim(order_padded, offsets[slot].astype(jnp.int32), window)
        valid = jnp.arange(window, dtype=jnp.int32) < counts[slot]
        feat_block = jnp.where(valid[:, None], features[rows], jnp.zeros((), jnp.bfloat16))
        target_block = jnp.where(valid[:, None], targets[rows], jnp.zeros((), jnp.bfloat16))
        predicted = jnp.dot(feat_block, slot_basis, preferred_element_type=jnp.float32)
        grad_corr = ((predicted - target_block.astype(jnp.float32)) * scale).astype(jnp.bfloat16)
        slot_grad = lax.dot_general(feat_block, grad_corr, (((0,), (0,)), ((), ())), preferred_element_type=jnp.float32).astype(jnp.bfloat16)
        back_rows = lax.dot_general(grad_corr, slot_basis, (((1,), (1,)), ((), ())), preferred_element_type=jnp.float32).astype(jnp.bfloat16)
        return slot_grad, back_rows

    grad_basis, back_all = lax.map(per_slot, (slots, basis))
    position = jnp.zeros((FRAMES,), jnp.int32).at[order].set(jnp.arange(FRAMES, dtype=jnp.int32))
    within = position - offsets[dest_slot]
    grad_feat = back_all[dest_slot, within]
    grad_w_out = lax.dot_general(hidden_two, grad_feat, (((0,), (0,)), ((), ())), preferred_element_type=jnp.float32)
    back_two = (lax.dot_general(grad_feat, w_out, (((1,), (1,)), ((), ())), preferred_element_type=jnp.float32) * silu_slope(pre_two)).astype(jnp.bfloat16)
    grad_w_hid = lax.dot_general(hidden_one, back_two, (((0,), (0,)), ((), ())), preferred_element_type=jnp.float32)
    back_one = (lax.dot_general(back_two, w_hid, (((1,), (1,)), ((), ())), preferred_element_type=jnp.float32) * silu_slope(pre_one)).astype(jnp.bfloat16)
    grad_w_in = lax.dot_general(pose_input, back_one, (((0,), (0,)), ((), ())), preferred_element_type=jnp.float32)
    return grad_w_in, grad_w_hid, grad_w_out, grad_basis
```

```python
import functools
import jax
import jax.numpy as jnp
from jax import lax
from jax.experimental import pallas as pl
from jax.experimental.pallas import tpu as pltpu
from jax.sharding import PartitionSpec as P

MESH = pl.DeviceIdType.MESH
F32, BF16 = jnp.float32, jnp.bfloat16
CHUNKS, CHUNK, PIECE = 7, 2304, 768
STRIDE = 45
LAST = CHUNKS - 1


def mm(left, right):
    return jnp.dot(left, right, preferred_element_type=F32)


def mm_t(left, right):
    return lax.dot_general(left, right, (((1,), (1,)), ((), ())), preferred_element_type=F32)


def silu_slope(value, sig):
    return sig * (1.0 + value * (1.0 - sig))


def place(me):
    return me // 32, (me // 8) % 4, (me // 2) % 4, me % 2


def device(z, y, x, c):
    return ((z * 4 + y) * 4 + x) * 2 + c


def peer(me, step):
    z, y, x, c = place(me)
    oz, oy, ox, oc = place((step * STRIDE) % 128)
    return device((z + oz) % 4, (y + oy) % 4, (x + ox) % 4, (c + oc) % 2)


def select_matrix(subject, owner):
    n = owner.shape[1]
    down = lax.broadcasted_iota(jnp.int32, (n, n), 0)
    across = lax.broadcasted_iota(jnp.int32, (n, n), 1)
    subject = jnp.broadcast_to(subject.astype(F32), (n, n))
    subject_row = jnp.sum(jnp.where(down == across, subject, 0.0), axis=0, keepdims=True)
    same = subject == subject_row
    rank = jnp.sum(jnp.where(same & (down < across), 1.0, 0.0), axis=0, keepdims=True)
    owner = jnp.broadcast_to(owner.astype(F32), (n, n))
    owner_col = jnp.sum(jnp.where(down == across, owner, 0.0), axis=1, keepdims=True)
    named = subject_row == down.astype(F32)
    slot = jnp.sum(jnp.where(named, owner_col, 0.0), axis=0, keepdims=True)
    row = 2.0 * slot + rank
    rows = lax.broadcasted_iota(jnp.int32, (2 * n, n), 0).astype(F32)
    return jnp.where(rows == row, 1.0, 0.0).astype(BF16)


def kernel(
    pose_h, tgt_h, basis_h, w_in, w_hid, w_out, subject, owner,
    gb_h, gwo, gwh, gwi,
    rows, basis, send, got, stage, pick, feat, feat_t, pose, h1_t, h2_t, slope1_t, slope2, grad_feat,
    parts, sums0, sums1, got0, got1, got2,
    load_sem, stage_sem, send_sem, got_sem, rs_send, rs_got,
):
    me = lax.axis_index("dev")
    z, y, x, c = place(me)
    width = tgt_h.shape[1]
    scale = width ** (-0.5)
    head = pose_h.shape[1]
    first = CHUNK - head

    loads = [
        pltpu.make_async_copy(pose_h, rows.at[:, 0:head], load_sem.at[0]),
        pltpu.make_async_copy(tgt_h.at[:, 0:first], rows.at[:, head:CHUNK], load_sem.at[1]),
        pltpu.make_async_copy(
            tgt_h.at[:, first:width], rows.at[:, CHUNK : head + width], load_sem.at[2]
        ),
        pltpu.make_async_copy(basis_h.at[0], basis.at[:, head : head + width], load_sem.at[3]),
    ]
    for load in loads:
        load.start()

    barrier = pltpu.get_barrier_semaphore()

    def greet(step, carry):
        pl.semaphore_signal(barrier, inc=1, device_id=(peer(me, step),), device_id_type=MESH)
        return carry

    lax.fori_loop(1, 128, greet, 0)

    rows[:, head + width :] = jnp.zeros((rows.shape[0], rows.shape[1] - head - width), BF16)
    basis[:, head + width :] = jnp.zeros((basis.shape[0], basis.shape[1] - head - width), BF16)
    basis[:, 0:head] = jnp.zeros((basis.shape[0], head), BF16)
    pick[...] = select_matrix(subject[...], owner[...])

    def fill(k):
        def piece(j, carry):
            at = pl.multiple_of(k * CHUNK + j * PIECE, 128)
            to = pl.multiple_of(j * PIECE, 128)
            block = mm(pick[...], rows[:, pl.ds(at, PIECE)]).astype(BF16)
            send[k, :, :, pl.ds(to, PIECE)] = block.reshape(128, 2, PIECE)
            return carry

        lax.fori_loop(0, CHUNK // PIECE, piece, 0)

    def ship(k):
        pltpu.make_async_copy(send.at[k, me], got.at[k, me], got_sem.at[k]).start()

        def one(step, carry):
            to = peer(me, step)
            pltpu.make_async_remote_copy(
                src_ref=send.at[k, to],
                dst_ref=got.at[k, me],
                send_sem=send_sem.at[k],
                recv_sem=got_sem.at[k],
                device_id=(to,),
                device_id_type=MESH,
            ).start()
            return carry

        lax.fori_loop(1, 128, one, 0)

    loads[0].wait()
    loads[1].wait()
    fill(0)
    pl.semaphore_wait(barrier, 127)
    ship(0)
    loads[2].wait()

    def more(k, carry):
        fill(k)
        ship(k)
        return carry

    lax.fori_loop(1, CHUNKS, more, 0)
    loads[3].wait()

    def arrived(k):
        pltpu.make_async_copy(got.at[k], got.at[k], got_sem.at[k]).wait()

    arrived(0)
    pose[...] = got[0, :, :, 0:head].reshape(256, head)
    pre_one = mm(pose[...], w_in[...])
    sig_one = jax.nn.sigmoid(pre_one)
    hidden_one = (pre_one * sig_one).astype(BF16)
    h1_t[...] = hidden_one.T
    slope1_t[...] = silu_slope(pre_one, sig_one).T
    pre_two = mm(hidden_one, w_hid[...])
    sig_two = jax.nn.sigmoid(pre_two)
    hidden_two = (pre_two * sig_two).astype(BF16)
    h2_t[...] = hidden_two.T
    slope2[...] = silu_slope(pre_two, sig_two)
    feat[...] = mm(hidden_two, w_out[...]).astype(BF16)
    feat_t[...] = feat[...].T
    grad_feat[...] = jnp.zeros_like(grad_feat)

    def correct(k):
        def piece(j, carry):
            at = pl.multiple_of(k * CHUNK + j * PIECE, 128)
            to = pl.multiple_of(j * PIECE, 128)
            slab = basis[:, pl.ds(at, PIECE)]
            target = got[k, :, :, pl.ds(to, PIECE)].reshape(256, PIECE)
            corr = ((mm(feat[...], slab) - target.astype(F32)) * scale).astype(BF16)
            stage[k % 2, :, pl.ds(to, PIECE)] = corr
            grad_feat[...] += mm_t(corr, slab)
            return carry

        lax.fori_loop(0, CHUNK // PIECE, piece, 0)

    def outer(k):
        def piece(j, carry):
            to = pl.multiple_of(j * PIECE, 128)
            corr = stage[k % 2, :, pl.ds(to, PIECE)]
            stage[k % 2, :, pl.ds(to, PIECE)] = mm(feat_t[...], corr).astype(BF16)
            return carry

        lax.fori_loop(0, CHUNK // PIECE, piece, 0)

    def store(k):
        if isinstance(k, int) and k == 0:
            return pltpu.make_async_copy(
                stage.at[0, :, head:CHUNK], gb_h.at[0, :, 0:first], stage_sem.at[0]
            )
        if isinstance(k, int) and k == LAST:
            size = width - (LAST * CHUNK - head)
            return pltpu.make_async_copy(
                stage.at[k % 2, :, 0:size],
                gb_h.at[0, :, LAST * CHUNK - head : width],
                stage_sem.at[k % 2],
            )
        at = pl.multiple_of(k * CHUNK - head, 128)
        return pltpu.make_async_copy(
            stage.at[k % 2], gb_h.at[0, :, pl.ds(at, CHUNK)], stage_sem.at[k % 2]
        )

    correct(0)
    outer(0)
    store(0).start()
    arrived(1)
    correct(1)
    outer(1)
    store(1).start()
    store(0).wait()

    def middle(k, carry):
        arrived(k)
        correct(k)
        outer(k)
        store(k).start()
        store(k - 1).wait()
        return carry

    lax.fori_loop(2, LAST, middle, 0)
    arrived(LAST)
    correct(LAST)

    grad = grad_feat[...].astype(BF16)
    back_two = (mm_t(grad, w_out[...]) * slope2[...]).astype(BF16)
    back_one_t = (mm_t(w_hid[...], back_two) * slope1_t[...]).astype(BF16)
    for third in range(3):
        if third == 0:
            upper = mm(h2_t[...], grad)
        else:
            upper = mm(h1_t[...], back_two[:, 256 * (third - 1) : 256 * third])
        if third == 2:
            lower = mm(back_one_t, pose[...])
        else:
            lower = mm(h1_t[...], back_two[:, 512 + 256 * third : 768 + 256 * third])
        both = jnp.concatenate([upper.reshape(128, 8, 256), lower.reshape(128, 8, 256)], axis=1)
        parts[third] = both.astype(BF16).reshape(64, 2, 16, 256)

    twin = device(z, y, x, 1 - c)
    copies0 = []
    for third in range(3):
        copies0.append(
            pltpu.make_async_remote_copy(
                src_ref=parts.at[third, :, 1 - c],
                dst_ref=got0.at[third],
                send_sem=rs_send.at[0, third],
                recv_sem=rs_got.at[0, third],
                device_id=(twin,),
                device_id_type=MESH,
            )
        )
        copies0[-1].start()
    outer(LAST)
    store(LAST).start()
    store(LAST - 1).wait()

    spots = (x, y, z)

    def along(third, value):
        zyx = [z, y, x]
        zyx[2 - third] = value
        return device(*zyx, c)

    def rows1(ref, third, value):
        view = ref.at[third]
        if third == 0:
            return view.at[:, :, value]
        if third == 1:
            return view.at[:, value]
        return view.at[value]

    copies1 = []
    for third in range(3):
        copies0[third].wait_recv()
        own = parts[third, :, c].astype(F32)
        sums0[third] = (own + got0[third].astype(F32)).astype(BF16).reshape(4, 4, 4, 16, 256)
        for hop in (1, 3, 2):
            value = (spots[third] + hop) % 4
            copy = pltpu.make_async_remote_copy(
                src_ref=rows1(sums0, third, value),
                dst_ref=got1.at[third, hop - 1],
                send_sem=rs_send.at[hop, third],
                recv_sem=rs_got.at[hop, third],
                device_id=(along(third, value),),
                device_id_type=MESH,
            )
            copy.start()
            copies1.append((third, copy))

    def plane(third, a, b):
        if third == 0:
            return device(a, b, x, c)
        if third == 1:
            return device(a, y, b, c)
        return device(z, a, b, c)

    mine = ((z, y), (z, x), (y, x))
    for third in range(3):
        for which, copy in copies1:
            if which == third:
                copy.wait_recv()
        if third == 0:
            own = sums0[third, :, :, x]
        elif third == 1:
            own = sums0[third, :, y]
        else:
            own = sums0[third, z]
        total = own.astype(F32)
        for hop in range(3):
            total = total + got1[third, hop].astype(F32)
        sums1[third] = total.astype(BF16)
        a0, b0 = mine[third]

        def one(step, carry, third=third, a0=a0, b0=b0):
            off = (step * 5) % 16
            a, b = (a0 + off // 4) % 4, (b0 + off % 4) % 4
            pltpu.make_async_remote_copy(
                src_ref=sums1.at[third, a, b],
                dst_ref=got2.at[third, off - 1],
                send_sem=rs_send.at[4, third],
                recv_sem=rs_got.at[4, third],
                device_id=(plane(third, a, b),),
                device_id_type=MESH,
            ).start()
            return carry

        lax.fori_loop(1, 16, one, 0)

    for third in range(3):
        pltpu.make_async_copy(got2.at[third], got2.at[third], rs_got.at[4, third]).wait()
        a0, b0 = mine[third]
        total = sums1[third, a0, b0].astype(F32)
        total = total + jnp.sum(got2[third].astype(F32), axis=0)
        upper, lower = total[0:8], total[8:16]
        if third == 0:
            gwo[...] = upper
        else:
            gwh[:, 256 * (third - 1) : 256 * third] = upper
        if third == 2:
            gwi[...] = lower
        else:
            gwh[:, 512 + 256 * third : 768 + 256 * third] = lower

    def sent(k, carry):
        sample = send.at[k, pl.ds(0, 127)]
        pltpu.make_async_copy(sample, sample, send_sem.at[k]).wait()
        return carry

    lax.fori_loop(0, CHUNKS, sent, 0)
    for copy in copies0:
        copy.wait_send()
    for _, copy in copies1:
        copy.wait_send()
    for third in range(3):
        pltpu.make_async_copy(got2.at[third], got2.at[third], rs_send.at[4, third]).wait()
    store(LAST).wait()


def on_device(pose_input, w_in, w_hid, w_out, targets, basis, owner, frame_subject):
    frames, p_size = pose_input.shape
    width = targets.shape[1]
    hidden = w_hid.shape[0]
    vmem = pl.BlockSpec(memory_space=pltpu.VMEM)
    hbm = pl.BlockSpec(memory_space=pl.ANY)
    padded = CHUNKS * CHUNK
    grad_basis, gwo, gwh, gwi = pl.pallas_call(
        kernel,
        out_shape=(
            jax.ShapeDtypeStruct(basis.shape, BF16),
            jax.ShapeDtypeStruct((8, p_size), F32),
            jax.ShapeDtypeStruct((8, hidden), F32),
            jax.ShapeDtypeStruct((8, p_size), F32),
        ),
        in_specs=[hbm, hbm, hbm, vmem, vmem, vmem, vmem, vmem],
        out_specs=(hbm, vmem, vmem, vmem),
        scratch_shapes=[
            pltpu.VMEM((frames, padded), BF16),
            pltpu.VMEM((p_size, padded), BF16),
            pltpu.VMEM((CHUNKS, 128, 2, CHUNK), BF16),
            pltpu.VMEM((CHUNKS, 128, 2, CHUNK), BF16),
            pltpu.VMEM((2, p_size, CHUNK), BF16),
            pltpu.VMEM((256, frames), BF16),
            pltpu.VMEM((256, p_size), BF16),
            pltpu.VMEM((p_size, 256), BF16),
            pltpu.VMEM((256, p_size), BF16),
            pltpu.VMEM((hidden, 256), BF16),
            pltpu.VMEM((hidden, 256), BF16),
            pltpu.VMEM((hidden, 256), F32),
            pltpu.VMEM((256, hidden), F32),
            pltpu.VMEM((256, p_size), F32),
            pltpu.VMEM((3, 64, 2, 16, 256), BF16),
            pltpu.VMEM((3, 4, 4, 4, 16, 256), BF16),
            pltpu.VMEM((3, 4, 4, 16, 256), BF16),
            pltpu.VMEM((3, 64, 16, 256), BF16),
            pltpu.VMEM((3, 3, 4, 4, 16, 256), BF16),
            pltpu.VMEM((3, 15, 16, 256), BF16),
            pltpu.SemaphoreType.DMA((4,)),
            pltpu.SemaphoreType.DMA((2,)),
            pltpu.SemaphoreType.DMA((CHUNKS,)),
            pltpu.SemaphoreType.DMA((CHUNKS,)),
            pltpu.SemaphoreType.DMA((5, 3)),
            pltpu.SemaphoreType.DMA((5, 3)),
        ],
        compiler_params=pltpu.CompilerParams(
            collective_id=0, has_side_effects=True, vmem_limit_bytes=60 * 2**20
        ),
    )(
        pose_input, targets, basis, w_in, w_hid, w_out,
        frame_subject.astype(jnp.int32), owner.astype(jnp.int32).reshape(1, -1),
    )
    return gwi.T, gwh, gwo, grad_basis


def solution(mesh):
    in_specs = (
        P("dev", None),
        P(),
        P(),
        P(),
        P("dev", None),
        P("dev", None, None),
        P(),
        P("dev", None),
    )
    out_specs = (P(None, "dev"), P("dev", None), P("dev", None), P("dev", None, None))
    return jax.shard_map(
        on_device, mesh=mesh, in_specs=in_specs, out_specs=out_specs, check_vma=False
    )
```

```python
import functools
import jax
import jax.numpy as jnp
from jax import lax
from jax.experimental import pallas as pl
from jax.experimental.pallas import tpu as pltpu
from jax.sharding import PartitionSpec as P

MESH = pl.DeviceIdType.MESH
F32, BF16 = jnp.float32, jnp.bfloat16
CHUNKS, CHUNK, PIECE = 7, 2304, 768
STRIDE = 37
LAST = CHUNKS - 1
VMEM_LIMIT = 54 * 2**20


def mm(left, right):
    return jnp.dot(left, right, preferred_element_type=F32)


def mm_t(left, right):
    return lax.dot_general(left, right, (((1,), (1,)), ((), ())), preferred_element_type=F32)


def silu_slope(value, sig):
    return sig * (1.0 + value * (1.0 - sig))


def device(z, y, x, c):
    return ((z * 4 + y) * 4 + x) * 2 + c


def peer(me, step):
    return lax.rem(me + step * STRIDE, 128)


def select_matrix(subject, owner):
    n = owner.shape[1]
    down = lax.broadcasted_iota(jnp.int32, (n, n), 0)
    across = lax.broadcasted_iota(jnp.int32, (n, n), 1)
    subject_row = subject.astype(F32)
    wide = jnp.broadcast_to(subject_row, (n, n))
    subject_col = jnp.sum(jnp.where(down == across, wide, 0.0), axis=1, keepdims=True)
    same = subject_col == subject_row
    rank = jnp.sum(jnp.where(same & (down < across), 1.0, 0.0), axis=0, keepdims=True)
    owner = jnp.broadcast_to(owner.astype(F32), (n, n))
    owner_col = jnp.sum(jnp.where(down == across, owner, 0.0), axis=1, keepdims=True)
    named = subject_row == down.astype(F32)
    slot = jnp.sum(jnp.where(named, owner_col, 0.0), axis=0, keepdims=True)
    row = 2.0 * slot + rank
    rows = lax.broadcasted_iota(jnp.int32, (2 * n, n), 0).astype(F32)
    return jnp.where(rows == row, 1.0, 0.0).astype(BF16)


def half_matrix(c, rows, columns):
    row = lax.broadcasted_iota(jnp.int32, (rows, columns), 0)
    column = lax.broadcasted_iota(jnp.int32, (rows, columns), 1)
    return jnp.where(column == 2 * row - row % 8 + 8 * c, 1.0, 0.0).astype(BF16)


def kernel(
    pose_h, tgt_h, basis_h, w_in, w_hid, w_out, subject, owner,
    gb, gwo, gwh, gwi,
    rows, basis, send, got, pick, feat, feat_t, pose, half, w_in_t, w_hid_half,
    h1_t, h2_t, slope1_t, slope2, grad_feat, grad, back_two, back_one_t,
    sums0, sums1, got1, got2,
    load_sem, send_sem, got_sem, rs_send, rs_got,
):
    me = lax.axis_index("dev")
    z, y, x, c = me // 32, (me // 8) % 4, (me // 2) % 4, me % 2
    width = tgt_h.shape[1]
    scale = width ** (-0.5)
    head = pose_h.shape[1]
    first = CHUNK - head
    rest = head + width - LAST * CHUNK

    loads = [
        pltpu.make_async_copy(pose_h, rows.at[:, 0:head], load_sem.at[0]),
        pltpu.make_async_copy(tgt_h.at[:, 0:first], rows.at[:, head:CHUNK], load_sem.at[1]),
        pltpu.make_async_copy(
            tgt_h.at[:, first:width], rows.at[:, CHUNK : head + width], load_sem.at[2]
        ),
        pltpu.make_async_copy(basis_h.at[0], basis.at[:, head : head + width], load_sem.at[3]),
    ]
    for load in loads:
        load.start()

    barrier = pltpu.get_barrier_semaphore()

    def greet(step, carry):
        pl.semaphore_signal(barrier, inc=1, device_id=(peer(me, step),), device_id_type=MESH)
        return carry

    lax.fori_loop(1, 128, greet, 0)

    rows[:, head + width :] = jnp.zeros((rows.shape[0], rows.shape[1] - head - width), BF16)
    basis[:, head + width :] = jnp.zeros((basis.shape[0], basis.shape[1] - head - width), BF16)
    basis[:, 0:head] = jnp.zeros((basis.shape[0], head), BF16)
    got[LAST, :, :, rest:] = jnp.zeros((128, 2, CHUNK - rest), BF16)
    pick[...] = select_matrix(subject[...], owner[...])

    def fill(k):
        def piece(j, carry):
            at = pl.multiple_of(k * CHUNK + j * PIECE, 128)
            to = pl.multiple_of(j * PIECE, 128)
            block = mm(pick[...], rows[:, pl.ds(at, PIECE)]).astype(BF16)
            send[k, :, :, pl.ds(to, PIECE)] = block.reshape(128, 2, PIECE)
            return carry

        lax.fori_loop(0, CHUNK // PIECE, piece, 0)

    def ship(k, size):
        pltpu.make_async_copy(
            send.at[k, me, :, 0:size], got.at[k, me, :, 0:size], got_sem.at[k]
        ).start()

        def one(step, carry):
            to = peer(me, step)
            pltpu.make_async_remote_copy(
                src_ref=send.at[k, to, :, 0:size],
                dst_ref=got.at[k, me, :, 0:size],
                send_sem=send_sem.at[k],
                recv_sem=got_sem.at[k],
                device_id=(to,),
                device_id_type=MESH,
            ).start()
            return carry

        lax.fori_loop(1, 128, one, 0)

    loads[0].wait()
    loads[1].wait()
    fill(0)
    pl.semaphore_wait(barrier, 127)
    ship(0, CHUNK)
    loads[2].wait()

    def more(k, carry):
        fill(k)
        ship(k, CHUNK)
        return carry

    lax.fori_loop(1, LAST, more, 0)
    fill(LAST)
    ship(LAST, rest)

    half[...] = half_matrix(c, half.shape[0], half.shape[1])
    w_in_t[...] = mm_t(half[...], w_in[...]).astype(BF16)
    w_hid_half[...] = mm(half[...], w_hid[...]).astype(BF16)
    loads[3].wait()

    def arrived(k, size):
        block = got.at[k, :, :, 0:size]
        pltpu.make_async_copy(block, block, got_sem.at[k]).wait()

    def forward(part):
        at = 256 * part
        pre_one = mm(pose[at : at + 256, :], w_in[...])
        hidden_one = (pre_one * jax.nn.sigmoid(pre_one)).astype(BF16)
        pre_two = mm(hidden_one, w_hid[...])
        sig_two = jax.nn.sigmoid(pre_two)
        hidden_two = (pre_two * sig_two).astype(BF16)
        slope2[at : at + 256, :] = silu_slope(pre_two, sig_two)
        h2_t[:, at : at + 256] = mm_t(half[...], hidden_two).astype(BF16)
        return hidden_two

    twin = device(z, y, x, 1 - c)

    def to_twin(ref, slot):
        return pltpu.make_async_remote_copy(
            src_ref=ref.at[0:256],
            dst_ref=ref.at[256:512],
            send_sem=rs_send.at[0, slot],
            recv_sem=rs_got.at[0, slot],
            device_id=(twin,),
            device_id_type=MESH,
        )

    arrived(0, CHUNK)
    pose[0:256, :] = got[0, :, :, 0:head].reshape(256, head)
    pose_copy = to_twin(pose, 0)
    pose_copy.start()
    feat[...] = mm(forward(0), w_out[...]).astype(BF16)
    feat_t[...] = feat[...].T
    grad_feat[...] = jnp.zeros_like(grad_feat)

    def correct(k):
        def piece(j, carry):
            at = pl.multiple_of(k * CHUNK + j * PIECE, 128)
            to = pl.multiple_of(j * PIECE, 128)
            slab = basis[:, pl.ds(at, PIECE)]
            target = got[k, :, :, pl.ds(to, PIECE)].reshape(256, PIECE)
            corr = ((mm(feat[...], slab) - target.astype(F32)) * scale).astype(BF16)
            gb[:, pl.ds(at, PIECE)] = corr
            grad_feat[...] += mm_t(corr, slab)
            return carry

        lax.fori_loop(0, CHUNK // PIECE, piece, 0)

    def outer(k):
        def piece(j, carry):
            at = pl.multiple_of(k * CHUNK + j * PIECE, 128)
            gb[:, pl.ds(at, PIECE)] = mm(feat_t[...], gb[:, pl.ds(at, PIECE)]).astype(BF16)
            return carry

        lax.fori_loop(0, CHUNK // PIECE, piece, 0)

    def turn(k, carry):
        arrived(k, CHUNK)
        correct(k)
        outer(k)
        return carry

    correct(0)
    outer(0)
    lax.fori_loop(1, 3, turn, 0)
    pose_copy.wait_recv()
    forward(1)
    pre_t = mm_t(w_in_t[...], pose[...])
    sig_t = jax.nn.sigmoid(pre_t)
    h1_t[...] = (pre_t * sig_t).astype(BF16)
    slope1_t[...] = silu_slope(pre_t, sig_t)
    lax.fori_loop(3, LAST, turn, 0)
    arrived(LAST, rest)
    correct(LAST)

    grad[0:256, :] = grad_feat[...].astype(BF16)
    grad_copy = to_twin(grad, 1)
    grad_copy.start()

    def backward(part):
        at = 256 * part
        back = mm_t(grad[at : at + 256, :], w_out[...]) * slope2[at : at + 256, :]
        back_two[at : at + 256, :] = back.astype(BF16)

    backward(0)
    grad_copy.wait_recv()
    backward(1)

    spots = (x, y, z)

    def along(third, value):
        zyx = [z, y, x]
        zyx[2 - third] = value
        return device(*zyx, c)

    def rows1(ref, third, value):
        view = ref.at[third]
        if third == 0:
            return view.at[:, :, value]
        if third == 1:
            return view.at[:, value]
        return view.at[value]

    copies1 = []
    for third in range(3):
        if third == 0:
            upper = mm(h2_t[...], grad[...])
        else:
            upper = mm(h1_t[...], back_two[:, 256 * (third - 1) : 256 * third])
        if third == 2:
            back = mm_t(w_hid_half[...], back_two[...]) * slope1_t[...]
            back_one_t[...] = back.astype(BF16)
            lower = mm(back_one_t[...], pose[...])
        else:
            lower = mm(h1_t[...], back_two[:, 512 + 256 * third : 768 + 256 * third])
        both = jnp.concatenate([upper.reshape(64, 8, 256), lower.reshape(64, 8, 256)], axis=1)
        sums0[third] = both.astype(BF16).reshape(4, 4, 4, 16, 256)
        for hop in (1, 3, 2):
            value = (spots[third] + hop) % 4
            copy = pltpu.make_async_remote_copy(
                src_ref=rows1(sums0, third, value),
                dst_ref=got1.at[third, hop - 1],
                send_sem=rs_send.at[hop, third],
                recv_sem=rs_got.at[hop, third],
                device_id=(along(third, value),),
                device_id_type=MESH,
            )
            copy.start()
            copies1.append((third, copy))
    outer(LAST)

    def plane(third, a, b):
        if third == 0:
            return device(a, b, x, c)
        if third == 1:
            return device(a, y, b, c)
        return device(z, a, b, c)

    mine = ((z, y), (z, x), (y, x))
    for third in range(3):
        for which, copy in copies1:
            if which == third:
                copy.wait_recv()
        if third == 0:
            own = sums0[third, :, :, x]
        elif third == 1:
            own = sums0[third, :, y]
        else:
            own = sums0[third, z]
        total = own.astype(F32)
        for hop in range(3):
            total = total + got1[third, hop].astype(F32)
        sums1[third] = total.astype(BF16)
        a0, b0 = mine[third]
        for off in (5, 15, 4, 1, 12, 3, 13, 7, 10, 8, 2, 6, 9, 14, 11):
            a, b = (a0 + off // 4) % 4, (b0 + off % 4) % 4
            pltpu.make_async_remote_copy(
                src_ref=sums1.at[third, a, b],
                dst_ref=got2.at[third, off - 1],
                send_sem=rs_send.at[4, third],
                recv_sem=rs_got.at[4, third],
                device_id=(plane(third, a, b),),
                device_id_type=MESH,
            ).start()

    for third in range(3):
        pltpu.make_async_copy(got2.at[third], got2.at[third], rs_got.at[4, third]).wait()
        a0, b0 = mine[third]
        total = sums1[third, a0, b0].astype(F32)
        total = total + jnp.sum(got2[third].astype(F32), axis=0)
        upper, lower = total[0:8], total[8:16]
        if third == 0:
            gwo[...] = upper
        else:
            gwh[:, 256 * (third - 1) : 256 * third] = upper
        if third == 2:
            gwi[...] = lower
        else:
            gwh[:, 512 + 256 * third : 768 + 256 * third] = lower

    def sent(k, size):
        sample = send.at[k, pl.ds(0, 127), :, 0:size]
        pltpu.make_async_copy(sample, sample, send_sem.at[k]).wait()

    def all_sent(k, carry):
        sent(k, CHUNK)
        return carry

    lax.fori_loop(0, LAST, all_sent, 0)
    sent(LAST, rest)
    pose_copy.wait_send()
    grad_copy.wait_send()
    for _, copy in copies1:
        copy.wait_send()
    for third in range(3):
        pltpu.make_async_copy(got2.at[third], got2.at[third], rs_send.at[4, third]).wait()


def deliver(head, gb, gwo, gwh, gwi, gb_h, gwo_h, gwh_h, gwi_h, sem):
    width = gb_h.shape[2]
    copies = [
        pltpu.make_async_copy(gb.at[:, head : head + width], gb_h.at[0], sem.at[0]),
        pltpu.make_async_copy(gwo, gwo_h, sem.at[1]),
        pltpu.make_async_copy(gwh, gwh_h, sem.at[2]),
        pltpu.make_async_copy(gwi, gwi_h, sem.at[3]),
    ]
    for copy in copies:
        copy.start()
    for copy in copies:
        copy.wait()


def on_device(pose_input, w_in, w_hid, w_out, targets, basis, owner, frame_subject):
    frames, p_size = pose_input.shape
    hidden = w_hid.shape[0]
    vmem = pl.BlockSpec(memory_space=pltpu.VMEM)
    hbm = pl.BlockSpec(memory_space=pl.ANY)
    padded = CHUNKS * CHUNK
    kept = pl.pallas_call(
        kernel,
        out_shape=(
            pltpu.VMEM((p_size, padded), BF16),
            pltpu.VMEM((8, p_size), F32),
            pltpu.VMEM((8, hidden), F32),
            pltpu.VMEM((8, p_size), F32),
        ),
        in_specs=[hbm, hbm, hbm, vmem, vmem, vmem, vmem, vmem],
        out_specs=(vmem, vmem, vmem, vmem),
        scratch_shapes=[
            pltpu.VMEM((frames, padded), BF16),
            pltpu.VMEM((p_size, padded), BF16),
            pltpu.VMEM((CHUNKS, 128, 2, CHUNK), BF16),
            pltpu.VMEM((CHUNKS, 128, 2, CHUNK), BF16),
            pltpu.VMEM((256, frames), BF16),
            pltpu.VMEM((256, p_size), BF16),
            pltpu.VMEM((p_size, 256), BF16),
            pltpu.VMEM((512, p_size), BF16),
            pltpu.VMEM((hidden // 2, hidden), BF16),
            pltpu.VMEM((hidden // 2, p_size), BF16),
            pltpu.VMEM((hidden // 2, hidden), BF16),
            pltpu.VMEM((hidden // 2, 512), BF16),
            pltpu.VMEM((hidden // 2, 512), BF16),
            pltpu.VMEM((hidden // 2, 512), F32),
            pltpu.VMEM((512, hidden), F32),
            pltpu.VMEM((256, p_size), F32),
            pltpu.VMEM((512, p_size), BF16),
            pltpu.VMEM((512, hidden), BF16),
            pltpu.VMEM((hidden // 2, 512), BF16),
            pltpu.VMEM((3, 4, 4, 4, 16, 256), BF16),
            pltpu.VMEM((3, 4, 4, 16, 256), BF16),
            pltpu.VMEM((3, 3, 4, 4, 16, 256), BF16),
            pltpu.VMEM((3, 15, 16, 256), BF16),
            pltpu.SemaphoreType.DMA((4,)),
            pltpu.SemaphoreType.DMA((CHUNKS,)),
            pltpu.SemaphoreType.DMA((CHUNKS,)),
            pltpu.SemaphoreType.DMA((5, 3)),
            pltpu.SemaphoreType.DMA((5, 3)),
        ],
        compiler_params=pltpu.CompilerParams(
            collective_id=0, has_side_effects=True, vmem_limit_bytes=VMEM_LIMIT
        ),
    )(
        pose_input, targets, basis, w_in, w_hid, w_out,
        frame_subject.astype(jnp.int32).reshape(1, -1), owner.astype(jnp.int32).reshape(1, -1),
    )
    grad_basis, gwo, gwh, gwi = pl.pallas_call(
        functools.partial(deliver, p_size),
        out_shape=(
            jax.ShapeDtypeStruct(basis.shape, BF16),
            jax.ShapeDtypeStruct((8, p_size), F32),
            jax.ShapeDtypeStruct((8, hidden), F32),
            jax.ShapeDtypeStruct((8, p_size), F32),
        ),
        in_specs=[hbm] * 4,
        out_specs=(hbm,) * 4,
        scratch_shapes=[pltpu.SemaphoreType.DMA((4,))],
        compiler_params=pltpu.CompilerParams(vmem_limit_bytes=2**20),
    )(*(pltpu.with_memory_space_constraint(value, pltpu.VMEM) for value in kept))
    return gwi.T, gwh, gwo, grad_basis


def solution(mesh):
    in_specs = (
        P("dev", None),
        P(),
        P(),
        P(),
        P("dev", None),
        P("dev", None, None),
        P(),
        P("dev", None),
    )
    out_specs = (P(None, "dev"), P("dev", None), P("dev", None), P("dev", None, None))
    return jax.shard_map(
        on_device, mesh=mesh, in_specs=in_specs, out_specs=out_specs, check_vma=False
    )
```

```python
import functools
import jax
import jax.numpy as jnp
from jax import lax
from jax.experimental import pallas as pl
from jax.experimental.pallas import tpu as pltpu
from jax.sharding import PartitionSpec as P

MESH = pl.DeviceIdType.MESH
F32, BF16 = jnp.float32, jnp.bfloat16
CHUNKS, CHUNK, PIECE = 7, 2304, 768
STRIDE = 37
LAST = CHUNKS - 1
VMEM_LIMIT = 54 * 2**20
BLOCKS = 4


def mm(left, right):
    return jnp.dot(left, right, preferred_element_type=F32)


def mm_t(left, right):
    return lax.dot_general(left, right, (((1,), (1,)), ((), ())), preferred_element_type=F32)


def silu_slope(value, sig):
    return sig * (1.0 + value * (1.0 - sig))


def device(z, y, x, c):
    return ((z * 4 + y) * 4 + x) * 2 + c


def peer(me, step):
    return lax.rem(me + step * STRIDE, 128)


def select_matrix(subject, owner):
    n = owner.shape[1]
    down = lax.broadcasted_iota(jnp.int32, (n, n), 0)
    across = lax.broadcasted_iota(jnp.int32, (n, n), 1)
    subject_row = subject.astype(F32)
    wide = jnp.broadcast_to(subject_row, (n, n))
    subject_col = jnp.sum(jnp.where(down == across, wide, 0.0), axis=1, keepdims=True)
    same = subject_col == subject_row
    rank = jnp.sum(jnp.where(same & (down < across), 1.0, 0.0), axis=0, keepdims=True)
    owner = jnp.broadcast_to(owner.astype(F32), (n, n))
    owner_col = jnp.sum(jnp.where(down == across, owner, 0.0), axis=1, keepdims=True)
    named = subject_row == down.astype(F32)
    slot = jnp.sum(jnp.where(named, owner_col, 0.0), axis=0, keepdims=True)
    row = 2.0 * slot + rank
    rows = lax.broadcasted_iota(jnp.int32, (2 * n, n), 0).astype(F32)
    return jnp.where(rows == row, 1.0, 0.0).astype(BF16)


def half_matrix(c, rows, columns):
    row = lax.broadcasted_iota(jnp.int32, (rows, columns), 0)
    column = lax.broadcasted_iota(jnp.int32, (rows, columns), 1)
    return jnp.where(column == 2 * row - row % 8 + 8 * c, 1.0, 0.0).astype(BF16)


def kernel(
    pose_h, tgt_h, basis_h, w_in_h, w_hid_h, w_out_h, subject_h, owner_h,
    gb, gwo, gwh, gwi,
    w_in, w_hid, w_out, subject, owner, rows, basis, send, got, pick, feat, feat_t, pose, half, w_in_t, w_hid_half,
    h1_t, h2_t, slope1_t, slope2, grad_feat, grad, back_two, back_one_t,
    halves, sums0, sums1, got1, got2,
    load_sem, send_sem, got_sem, rs_send, rs_got,
):
    me = lax.axis_index("dev")
    z, y, x, c = me // 32, (me // 8) % 4, (me // 2) % 4, me % 2
    width = tgt_h.shape[1]
    scale = width ** (-0.5)
    head = pose_h.shape[1]
    first = CHUNK - head
    rest = head + width - LAST * CHUNK

    pairs = [
        (subject_h, subject),
        (owner_h, owner),
        (pose_h, rows.at[:, 0:head]),
        (tgt_h.at[:, 0:first], rows.at[:, head:CHUNK]),
        (tgt_h.at[:, first:width], rows.at[:, CHUNK : head + width]),
        (w_in_h, w_in),
        (w_hid_h, w_hid),
        (w_out_h, w_out),
        (basis_h.at[0], basis.at[:, head : head + width]),
    ]
    loads = [
        pltpu.make_async_copy(src, dst, load_sem.at[at]) for at, (src, dst) in enumerate(pairs)
    ]
    for load in loads[:4]:
        load.start()

    barrier = pltpu.get_barrier_semaphore()

    def greet(step, carry):
        pl.semaphore_signal(barrier, inc=1, device_id=(peer(me, step),), device_id_type=MESH)
        return carry

    lax.fori_loop(1, 128, greet, 0)
    for load in loads[4:]:
        load.start()

    rows[:, head + width :] = jnp.zeros((rows.shape[0], rows.shape[1] - head - width), BF16)
    basis[:, head + width :] = jnp.zeros((basis.shape[0], basis.shape[1] - head - width), BF16)
    basis[:, 0:head] = jnp.zeros((basis.shape[0], head), BF16)
    got[LAST, :, :, rest:] = jnp.zeros((128, 2, CHUNK - rest), BF16)
    loads[0].wait()
    loads[1].wait()
    pick[...] = select_matrix(subject[...], owner[...])

    def fill(k):
        def piece(j, carry):
            at = pl.multiple_of(k * CHUNK + j * PIECE, 128)
            to = pl.multiple_of(j * PIECE, 128)
            block = mm(pick[...], rows[:, pl.ds(at, PIECE)]).astype(BF16)
            send[k, :, :, pl.ds(to, PIECE)] = block.reshape(128, 2, PIECE)
            return carry

        lax.fori_loop(0, CHUNK // PIECE, piece, 0)

    def ship(k, size):
        pltpu.make_async_copy(
            send.at[k, me, :, 0:size], got.at[k, me, :, 0:size], got_sem.at[k]
        ).start()

        def one(step, carry):
            to = peer(me, step)
            pltpu.make_async_remote_copy(
                src_ref=send.at[k, to, :, 0:size],
                dst_ref=got.at[k, me, :, 0:size],
                send_sem=send_sem.at[k],
                recv_sem=got_sem.at[k],
                device_id=(to,),
                device_id_type=MESH,
            ).start()
            return carry

        lax.fori_loop(1, 128, one, 0)

    loads[2].wait()
    loads[3].wait()
    fill(0)
    pl.semaphore_wait(barrier, 127)
    ship(0, CHUNK)
    loads[4].wait()

    def more(k, carry):
        fill(k)
        ship(k, CHUNK)
        return carry

    lax.fori_loop(1, LAST, more, 0)
    fill(LAST)
    ship(LAST, rest)

    for load in loads[5:]:
        load.wait()
    half[...] = half_matrix(c, half.shape[0], half.shape[1])
    w_in_t[...] = mm_t(half[...], w_in[...]).astype(BF16)
    w_hid_half[...] = mm(half[...], w_hid[...]).astype(BF16)

    def arrived(k, size):
        block = got.at[k, :, :, 0:size]
        pltpu.make_async_copy(block, block, got_sem.at[k]).wait()

    def forward(part):
        at = 256 * part
        pre_one = mm(pose[at : at + 256, :], w_in[...])
        hidden_one = (pre_one * jax.nn.sigmoid(pre_one)).astype(BF16)
        pre_two = mm(hidden_one, w_hid[...])
        sig_two = jax.nn.sigmoid(pre_two)
        hidden_two = (pre_two * sig_two).astype(BF16)
        slope2[at : at + 256, :] = silu_slope(pre_two, sig_two)
        h2_t[:, at : at + 256] = mm_t(half[...], hidden_two).astype(BF16)
        return hidden_two

    twin = device(z, y, x, 1 - c)

    def to_twin(ref, slot):
        return pltpu.make_async_remote_copy(
            src_ref=ref.at[0:256],
            dst_ref=ref.at[256:512],
            send_sem=rs_send.at[0, slot],
            recv_sem=rs_got.at[0, slot],
            device_id=(twin,),
            device_id_type=MESH,
        )

    arrived(0, CHUNK)
    pose[0:256, :] = got[0, :, :, 0:head].reshape(256, head)
    pose_copy = to_twin(pose, 0)
    pose_copy.start()
    feat[...] = mm(forward(0), w_out[...]).astype(BF16)
    feat_t[...] = feat[...].T
    grad_feat[...] = jnp.zeros_like(grad_feat)

    def correct(k, unroll=False):
        def piece(j, carry):
            at = pl.multiple_of(k * CHUNK + j * PIECE, 128)
            to = pl.multiple_of(j * PIECE, 128)
            slab = basis[:, pl.ds(at, PIECE)]
            target = got[k, :, :, pl.ds(to, PIECE)].reshape(256, PIECE)
            corr = ((mm(feat[...], slab) - target.astype(F32)) * scale).astype(BF16)
            gb[:, pl.ds(at, PIECE)] = corr
            grad_feat[...] += mm_t(corr, slab)
            return carry

        lax.fori_loop(0, CHUNK // PIECE, piece, 0, unroll=unroll)

    def outer(k):
        def piece(j, carry):
            at = pl.multiple_of(k * CHUNK + j * PIECE, 128)
            gb[:, pl.ds(at, PIECE)] = mm(feat_t[...], gb[:, pl.ds(at, PIECE)]).astype(BF16)
            return carry

        lax.fori_loop(0, CHUNK // PIECE, piece, 0)

    def turn(k, carry):
        arrived(k, CHUNK)
        correct(k)
        outer(k)
        return carry

    correct(0)
    outer(0)
    lax.fori_loop(1, 3, turn, 0)
    pose_copy.wait_recv()
    forward(1)
    pre_t = mm_t(w_in_t[...], pose[...])
    sig_t = jax.nn.sigmoid(pre_t)
    h1_t[...] = (pre_t * sig_t).astype(BF16)
    slope1_t[...] = silu_slope(pre_t, sig_t)
    lax.fori_loop(3, LAST, turn, 0)
    arrived(LAST, rest)
    correct(LAST, unroll=True)

    grad[0:256, :] = grad_feat[...].astype(BF16)
    grad_copy = to_twin(grad, 1)
    grad_copy.start()

    def backward(part):
        at = 256 * part
        back = mm_t(grad[at : at + 256, :], w_out[...]) * slope2[at : at + 256, :]
        back_two[at : at + 256, :] = back.astype(BF16)

    def product(third, lower, part):
        at = slice(256 * part, 256 * part + 256)
        if (third, lower) == (0, False):
            return mm(h2_t[:, at], grad[at, :])
        if (third, lower) == (2, True):
            back = mm_t(w_hid_half[...], back_two[at, :]) * slope1_t[:, at]
            back_one_t[...] = back.astype(BF16)
            return mm(back_one_t[...], pose[at, :])
        first_column = 256 * (third - 1) + (768 if lower else 0)
        return mm(h1_t[:, at], back_two[at, first_column : first_column + 256])

    backward(0)
    for third in range(3):
        for lower in (False, True):
            halves[2 * third + lower] = product(third, lower, 0)
    grad_copy.wait_recv()
    backward(1)

    spots = (x, y, z)

    def along(third, value):
        zyx = [z, y, x]
        zyx[2 - third] = value
        return device(*zyx, c)

    def rows1(ref, third, value):
        view = ref.at[third]
        if third == 0:
            return view.at[:, :, value]
        if third == 1:
            return view.at[:, value]
        return view.at[value]

    copies1 = []
    for third in range(3):
        upper = halves[2 * third] + product(third, False, 1)
        lower = halves[2 * third + 1] + product(third, True, 1)
        both = jnp.concatenate([upper.reshape(64, 8, 256), lower.reshape(64, 8, 256)], axis=1)
        sums0[third] = both.astype(BF16).reshape(4, 4, 4, 16, 256)
        for hop in (1, 3, 2):
            value = (spots[third] + hop) % 4
            copy = pltpu.make_async_remote_copy(
                src_ref=rows1(sums0, third, value),
                dst_ref=got1.at[third, hop - 1],
                send_sem=rs_send.at[hop, third],
                recv_sem=rs_got.at[hop, third],
                device_id=(along(third, value),),
                device_id_type=MESH,
            )
            copy.start()
            copies1.append((third, copy))
    outer(LAST)

    def plane(third, a, b):
        if third == 0:
            return device(a, b, x, c)
        if third == 1:
            return device(a, y, b, c)
        return device(z, a, b, c)

    mine = ((z, y), (z, x), (y, x))
    for third in range(3):
        for which, copy in copies1:
            if which == third:
                copy.wait_recv()
        if third == 0:
            own = sums0[third, :, :, x]
        elif third == 1:
            own = sums0[third, :, y]
        else:
            own = sums0[third, z]
        total = own.astype(F32)
        for hop in range(3):
            total = total + got1[third, hop].astype(F32)
        sums1[third] = total.astype(BF16)
        a0, b0 = mine[third]
        for off in (5, 15, 4, 1, 12, 3, 13, 7, 10, 8, 2, 6, 9, 14, 11):
            a, b = (a0 + off // 4) % 4, (b0 + off % 4) % 4
            pltpu.make_async_remote_copy(
                src_ref=sums1.at[third, a, b],
                dst_ref=got2.at[third, off - 1],
                send_sem=rs_send.at[4, third],
                recv_sem=rs_got.at[4, third],
                device_id=(plane(third, a, b),),
                device_id_type=MESH,
            ).start()

    for third in range(3):
        pltpu.make_async_copy(got2.at[third], got2.at[third], rs_got.at[4, third]).wait()
        a0, b0 = mine[third]
        total = sums1[third, a0, b0].astype(F32)
        total = total + jnp.sum(got2[third].astype(F32), axis=0)
        upper, lower = total[0:8], total[8:16]
        if third == 0:
            gwo[...] = upper
        else:
            gwh[:, 256 * (third - 1) : 256 * third] = upper
        if third == 2:
            gwi[...] = lower
        else:
            gwh[:, 512 + 256 * third : 768 + 256 * third] = lower

    def sent(k, size):
        sample = send.at[k, pl.ds(0, 127), :, 0:size]
        pltpu.make_async_copy(sample, sample, send_sem.at[k]).wait()

    def all_sent(k, carry):
        sent(k, CHUNK)
        return carry

    lax.fori_loop(0, LAST, all_sent, 0)
    sent(LAST, rest)
    pose_copy.wait_send()
    grad_copy.wait_send()
    for _, copy in copies1:
        copy.wait_send()
    for third in range(3):
        pltpu.make_async_copy(got2.at[third], got2.at[third], rs_send.at[4, third]).wait()


def deliver(head, gb, gwo, gwh, gwi, gb_h, gwo_h, gwh_h, gwi_h, sem):
    width = gb_h.shape[2]
    step = gb.shape[0] // BLOCKS
    copies = [
        pltpu.make_async_copy(gwo, gwo_h, sem.at[BLOCKS]),
        pltpu.make_async_copy(gwh, gwh_h, sem.at[BLOCKS + 1]),
        pltpu.make_async_copy(gwi, gwi_h, sem.at[BLOCKS + 2]),
    ]
    for block in range(BLOCKS):
        here = slice(block * step, block * step + step)
        copies.append(
            pltpu.make_async_copy(
                gb.at[here, head : head + width], gb_h.at[0, here], sem.at[block]
            )
        )
    for copy in copies:
        copy.start()
    for copy in copies:
        copy.wait()


def on_device(pose_input, w_in, w_hid, w_out, targets, basis, owner, frame_subject):
    frames, p_size = pose_input.shape
    hidden = w_hid.shape[0]
    vmem = pl.BlockSpec(memory_space=pltpu.VMEM)
    hbm = pl.BlockSpec(memory_space=pl.ANY)
    padded = CHUNKS * CHUNK
    kept = pl.pallas_call(
        kernel,
        out_shape=(
            pltpu.VMEM((p_size, padded), BF16),
            pltpu.VMEM((8, p_size), F32),
            pltpu.VMEM((8, hidden), F32),
            pltpu.VMEM((8, p_size), F32),
        ),
        in_specs=[hbm] * 8,
        out_specs=(vmem, vmem, vmem, vmem),
        scratch_shapes=[
            pltpu.VMEM(w_in.shape, BF16),
            pltpu.VMEM(w_hid.shape, BF16),
            pltpu.VMEM(w_out.shape, BF16),
            pltpu.VMEM((1, frames), jnp.int32),
            pltpu.VMEM((1, owner.shape[0]), jnp.int32),
            pltpu.VMEM((frames, padded), BF16),
            pltpu.VMEM((p_size, padded), BF16),
            pltpu.VMEM((CHUNKS, 128, 2, CHUNK), BF16),
            pltpu.VMEM((CHUNKS, 128, 2, CHUNK), BF16),
            pltpu.VMEM((256, frames), BF16),
            pltpu.VMEM((256, p_size), BF16),
            pltpu.VMEM((p_size, 256), BF16),
            pltpu.VMEM((512, p_size), BF16),
            pltpu.VMEM((hidden // 2, hidden), BF16),
            pltpu.VMEM((hidden // 2, p_size), BF16),
            pltpu.VMEM((hidden // 2, hidden), BF16),
            pltpu.VMEM((hidden // 2, 512), BF16),
            pltpu.VMEM((hidden // 2, 512), BF16),
            pltpu.VMEM((hidden // 2, 512), F32),
            pltpu.VMEM((512, hidden), F32),
            pltpu.VMEM((256, p_size), F32),
            pltpu.VMEM((512, p_size), BF16),
            pltpu.VMEM((512, hidden), BF16),
            pltpu.VMEM((hidden // 2, 256), BF16),
            pltpu.VMEM((6, hidden // 2, 256), F32),
            pltpu.VMEM((3, 4, 4, 4, 16, 256), BF16),
            pltpu.VMEM((3, 4, 4, 16, 256), BF16),
            pltpu.VMEM((3, 3, 4, 4, 16, 256), BF16),
            pltpu.VMEM((3, 15, 16, 256), BF16),
            pltpu.SemaphoreType.DMA((9,)),
            pltpu.SemaphoreType.DMA((CHUNKS,)),
            pltpu.SemaphoreType.DMA((CHUNKS,)),
            pltpu.SemaphoreType.DMA((5, 3)),
            pltpu.SemaphoreType.DMA((5, 3)),
        ],
        compiler_params=pltpu.CompilerParams(
            collective_id=0, has_side_effects=True, vmem_limit_bytes=VMEM_LIMIT
        ),
    )(
        pose_input, targets, basis, w_in, w_hid, w_out,
        frame_subject.astype(jnp.int32).reshape(1, -1), owner.astype(jnp.int32).reshape(1, -1),
    )
    grad_basis, gwo, gwh, gwi = pl.pallas_call(
        functools.partial(deliver, p_size),
        out_shape=(
            jax.ShapeDtypeStruct(basis.shape, BF16),
            jax.ShapeDtypeStruct((8, p_size), F32),
            jax.ShapeDtypeStruct((8, hidden), F32),
            jax.ShapeDtypeStruct((8, p_size), F32),
        ),
        in_specs=[hbm] * 4,
        out_specs=(hbm,) * 4,
        scratch_shapes=[pltpu.SemaphoreType.DMA((BLOCKS + 3,))],
        compiler_params=pltpu.CompilerParams(vmem_limit_bytes=2**20),
    )(*(pltpu.with_memory_space_constraint(value, pltpu.VMEM) for value in kept))
    return gwi.T, gwh, gwo, grad_basis


def solution(mesh):
    in_specs = (
        P("dev", None),
        P(),
        P(),
        P(),
        P("dev", None),
        P("dev", None, None),
        P(),
        P("dev", None),
    )
    out_specs = (P(None, "dev"), P("dev", None), P("dev", None), P("dev", None, None))
    return jax.shard_map(
        on_device, mesh=mesh, in_specs=in_specs, out_specs=out_specs, check_vma=False
    )
```

```python
import functools
import jax
import jax.numpy as jnp
from jax import lax
from jax.experimental import pallas as pl
from jax.experimental.pallas import tpu as pltpu
from jax.sharding import PartitionSpec as P

MESH = pl.DeviceIdType.MESH
F32, BF16 = jnp.float32, jnp.bfloat16
CHUNKS, CHUNK, PIECE = 7, 2304, 768
STRIDE = 37
LAST = CHUNKS - 1
VMEM_LIMIT = 54 * 2**20
BLOCKS = 4


def mm(left, right):
    return jnp.dot(left, right, preferred_element_type=F32)


def mm_t(left, right):
    return lax.dot_general(left, right, (((1,), (1,)), ((), ())), preferred_element_type=F32)


def silu_slope(value, sig):
    return sig * (1.0 + value * (1.0 - sig))


def device(z, y, x, c):
    return ((z * 4 + y) * 4 + x) * 2 + c


def peer(me, step):
    return lax.rem(me + step * STRIDE, 128)


def select_matrix(subject, owner):
    n = owner.shape[1]
    down = lax.broadcasted_iota(jnp.int32, (n, n), 0)
    across = lax.broadcasted_iota(jnp.int32, (n, n), 1)
    subject_row = subject.astype(F32)
    wide = jnp.broadcast_to(subject_row, (n, n))
    subject_col = jnp.sum(jnp.where(down == across, wide, 0.0), axis=1, keepdims=True)
    same = subject_col == subject_row
    rank = jnp.sum(jnp.where(same & (down < across), 1.0, 0.0), axis=0, keepdims=True)
    owner = jnp.broadcast_to(owner.astype(F32), (n, n))
    owner_col = jnp.sum(jnp.where(down == across, owner, 0.0), axis=1, keepdims=True)
    named = subject_row == down.astype(F32)
    slot = jnp.sum(jnp.where(named, owner_col, 0.0), axis=0, keepdims=True)
    row = 2.0 * slot + rank
    rows = lax.broadcasted_iota(jnp.int32, (2 * n, n), 0).astype(F32)
    return jnp.where(rows == row, 1.0, 0.0).astype(BF16)


def half_matrix(c, rows, columns):
    row = lax.broadcasted_iota(jnp.int32, (rows, columns), 0)
    column = lax.broadcasted_iota(jnp.int32, (rows, columns), 1)
    return jnp.where(column == 2 * row - row % 8 + 8 * c, 1.0, 0.0).astype(BF16)


def kernel(
    pose_h, tgt_h, basis_h, w_in_h, w_hid_h, w_out_h, subject_h, owner_h,
    gb, gwo, gwh, gwi,
    w_in, w_hid, w_out, subject, owner, rows, basis, send, got, pick, feat, feat_t, pose, half, w_in_t, w_hid_half,
    h1_t, h2_t, slope1_t, slope2, grad_feat, grad, back_two, back_one_t,
    halves, sums0, sums1, got1, got2,
    load_sem, send_sem, got_sem, rs_send, rs_got, vouched,
):
    me = lax.axis_index("dev")
    z, y, x, c = me // 32, (me // 8) % 4, (me // 2) % 4, me % 2
    width = tgt_h.shape[1]
    scale = width ** (-0.5)
    head = pose_h.shape[1]
    first = CHUNK - head
    rest = head + width - LAST * CHUNK

    pairs = [
        (subject_h, subject),
        (owner_h, owner),
        (pose_h, rows.at[:, 0:head]),
        (tgt_h.at[:, 0:first], rows.at[:, head:CHUNK]),
        (tgt_h.at[:, first:width], rows.at[:, CHUNK : head + width]),
        (w_in_h, w_in),
        (w_hid_h, w_hid),
        (w_out_h, w_out),
        (basis_h.at[0], basis.at[:, head : head + width]),
    ]
    loads = [
        pltpu.make_async_copy(src, dst, load_sem.at[at]) for at, (src, dst) in enumerate(pairs)
    ]
    for load in loads[:4]:
        load.start()

    barrier = pltpu.get_barrier_semaphore()

    line, block_of = me % 8, me // 8

    def mate(step):
        return block_of * 8 + lax.rem(line + step, 8)

    def across(step):
        return lax.rem(block_of + step, 16) * 8 + line

    def greet_across(step, carry):
        pl.semaphore_signal(barrier, inc=1, device_id=(across(step),), device_id_type=MESH)
        return carry

    def greet_mate(step, carry):
        pl.semaphore_signal(barrier, inc=1, device_id=(mate(step),), device_id_type=MESH)
        return carry

    def vouch(step, carry):
        pl.semaphore_signal(vouched, inc=1, device_id=(mate(step),), device_id_type=MESH)
        return carry

    lax.fori_loop(1, 16, greet_across, 0)
    lax.fori_loop(1, 8, greet_mate, 0)
    for load in loads[4:]:
        load.start()

    rows[:, head + width :] = jnp.zeros((rows.shape[0], rows.shape[1] - head - width), BF16)
    basis[:, head + width :] = jnp.zeros((basis.shape[0], basis.shape[1] - head - width), BF16)
    basis[:, 0:head] = jnp.zeros((basis.shape[0], head), BF16)
    got[LAST, :, :, rest:] = jnp.zeros((128, 2, CHUNK - rest), BF16)
    loads[0].wait()
    loads[1].wait()
    pick[...] = select_matrix(subject[...], owner[...])

    def fill(k):
        def piece(j, carry):
            at = pl.multiple_of(k * CHUNK + j * PIECE, 128)
            to = pl.multiple_of(j * PIECE, 128)
            block = mm(pick[...], rows[:, pl.ds(at, PIECE)]).astype(BF16)
            send[k, :, :, pl.ds(to, PIECE)] = block.reshape(128, 2, PIECE)
            return carry

        lax.fori_loop(0, CHUNK // PIECE, piece, 0)

    def ship_to(k, size, to):
        pltpu.make_async_remote_copy(
            src_ref=send.at[k, to, :, 0:size],
            dst_ref=got.at[k, me, :, 0:size],
            send_sem=send_sem.at[k],
            recv_sem=got_sem.at[k],
            device_id=(to,),
            device_id_type=MESH,
        ).start()

    def keep(k, size):
        pltpu.make_async_copy(
            send.at[k, me, :, 0:size], got.at[k, me, :, 0:size], got_sem.at[k]
        ).start()

    def ship(k, size):
        keep(k, size)

        def one(step, carry):
            ship_to(k, size, peer(me, step))
            return carry

        lax.fori_loop(1, 128, one, 0)

    def first_across(step, carry):
        ship_to(0, CHUNK, across(lax.rem(step * 4, 15) + 1))
        return carry

    def first_mate(step, carry):
        ship_to(0, CHUNK, mate(step))
        return carry

    def first_others(step, carry):
        to = lax.rem(block_of + 1 + lax.rem(step, 15), 16) * 8
        ship_to(0, CHUNK, to + lax.rem(line + 1 + lax.rem(step, 7), 8))
        return carry

    loads[2].wait()
    loads[3].wait()
    fill(0)
    pl.semaphore_wait(barrier, 22)
    lax.fori_loop(1, 8, vouch, 0)
    keep(0, CHUNK)
    lax.fori_loop(0, 15, first_across, 0)
    lax.fori_loop(1, 8, first_mate, 0)
    pl.semaphore_wait(vouched, 7)
    lax.fori_loop(0, 105, first_others, 0)
    loads[4].wait()

    def more(k, carry):
        fill(k)
        ship(k, CHUNK)
        return carry

    lax.fori_loop(1, LAST, more, 0)
    fill(LAST)
    ship(LAST, rest)

    for load in loads[5:]:
        load.wait()
    half[...] = half_matrix(c, half.shape[0], half.shape[1])
    w_in_t[...] = mm_t(half[...], w_in[...]).astype(BF16)
    w_hid_half[...] = mm(half[...], w_hid[...]).astype(BF16)

    def arrived(k, size):
        block = got.at[k, :, :, 0:size]
        pltpu.make_async_copy(block, block, got_sem.at[k]).wait()

    def forward(part):
        at = 256 * part
        pre_one = mm(pose[at : at + 256, :], w_in[...])
        hidden_one = (pre_one * jax.nn.sigmoid(pre_one)).astype(BF16)
        pre_two = mm(hidden_one, w_hid[...])
        sig_two = jax.nn.sigmoid(pre_two)
        hidden_two = (pre_two * sig_two).astype(BF16)
        slope2[at : at + 256, :] = silu_slope(pre_two, sig_two)
        h2_t[:, at : at + 256] = mm_t(half[...], hidden_two).astype(BF16)
        return hidden_two

    twin = device(z, y, x, 1 - c)

    def to_twin(ref, slot):
        return pltpu.make_async_remote_copy(
            src_ref=ref.at[0:256],
            dst_ref=ref.at[256:512],
            send_sem=rs_send.at[0, slot],
            recv_sem=rs_got.at[0, slot],
            device_id=(twin,),
            device_id_type=MESH,
        )

    arrived(0, CHUNK)
    pose[0:256, :] = got[0, :, :, 0:head].reshape(256, head)
    pose_copy = to_twin(pose, 0)
    pose_copy.start()
    feat[...] = mm(forward(0), w_out[...]).astype(BF16)
    feat_t[...] = feat[...].T
    grad_feat[...] = jnp.zeros_like(grad_feat)

    def correct(k, unroll=False):
        def piece(j, carry):
            at = pl.multiple_of(k * CHUNK + j * PIECE, 128)
            to = pl.multiple_of(j * PIECE, 128)
            slab = basis[:, pl.ds(at, PIECE)]
            target = got[k, :, :, pl.ds(to, PIECE)].reshape(256, PIECE)
            corr = ((mm(feat[...], slab) - target.astype(F32)) * scale).astype(BF16)
            gb[:, pl.ds(at, PIECE)] = corr
            grad_feat[...] += mm_t(corr, slab)
            return carry

        lax.fori_loop(0, CHUNK // PIECE, piece, 0, unroll=unroll)

    def outer(k):
        def piece(j, carry):
            at = pl.multiple_of(k * CHUNK + j * PIECE, 128)
            gb[:, pl.ds(at, PIECE)] = mm(feat_t[...], gb[:, pl.ds(at, PIECE)]).astype(BF16)
            return carry

        lax.fori_loop(0, CHUNK // PIECE, piece, 0)

    def turn(k, carry):
        arrived(k, CHUNK)
        correct(k)
        outer(k)
        return carry

    correct(0)
    outer(0)
    lax.fori_loop(1, 3, turn, 0)
    pose_copy.wait_recv()
    forward(1)
    pre_t = mm_t(w_in_t[...], pose[...])
    sig_t = jax.nn.sigmoid(pre_t)
    h1_t[...] = (pre_t * sig_t).astype(BF16)
    slope1_t[...] = silu_slope(pre_t, sig_t)
    lax.fori_loop(3, LAST, turn, 0)
    arrived(LAST, rest)
    correct(LAST, unroll=True)

    grad[0:256, :] = grad_feat[...].astype(BF16)
    grad_copy = to_twin(grad, 1)
    grad_copy.start()

    def backward(part):
        at = 256 * part
        back = mm_t(grad[at : at + 256, :], w_out[...]) * slope2[at : at + 256, :]
        back_two[at : at + 256, :] = back.astype(BF16)

    def product(third, lower, part):
        at = slice(256 * part, 256 * part + 256)
        if (third, lower) == (0, False):
            return mm(h2_t[:, at], grad[at, :])
        if (third, lower) == (2, True):
            back = mm_t(w_hid_half[...], back_two[at, :]) * slope1_t[:, at]
            back_one_t[...] = back.astype(BF16)
            return mm(back_one_t[...], pose[at, :])
        first_column = 256 * (third - 1) + (768 if lower else 0)
        return mm(h1_t[:, at], back_two[at, first_column : first_column + 256])

    backward(0)
    for third in range(3):
        for lower in (False, True):
            halves[2 * third + lower] = product(third, lower, 0)
    grad_copy.wait_recv()
    backward(1)

    spots = (x, y, z)

    def along(third, value):
        zyx = [z, y, x]
        zyx[2 - third] = value
        return device(*zyx, c)

    def rows1(ref, third, value):
        view = ref.at[third]
        if third == 0:
            return view.at[:, :, value]
        if third == 1:
            return view.at[:, value]
        return view.at[value]

    copies1 = []
    for third in range(3):
        upper = halves[2 * third] + product(third, False, 1)
        lower = halves[2 * third + 1] + product(third, True, 1)
        both = jnp.concatenate([upper.reshape(64, 8, 256), lower.reshape(64, 8, 256)], axis=1)
        sums0[third] = both.astype(BF16).reshape(4, 4, 4, 16, 256)
        for hop in (1, 3, 2):
            value = (spots[third] + hop) % 4
            copy = pltpu.make_async_remote_copy(
                src_ref=rows1(sums0, third, value),
                dst_ref=got1.at[third, hop - 1],
                send_sem=rs_send.at[hop, third],
                recv_sem=rs_got.at[hop, third],
                device_id=(along(third, value),),
                device_id_type=MESH,
            )
            copy.start()
            copies1.append((third, copy))
    outer(LAST)

    def plane(third, a, b):
        if third == 0:
            return device(a, b, x, c)
        if third == 1:
            return device(a, y, b, c)
        return device(z, a, b, c)

    mine = ((z, y), (z, x), (y, x))
    for third in range(3):
        for which, copy in copies1:
            if which == third:
                copy.wait_recv()
        if third == 0:
            own = sums0[third, :, :, x]
        elif third == 1:
            own = sums0[third, :, y]
        else:
            own = sums0[third, z]
        total = own.astype(F32)
        for hop in range(3):
            total = total + got1[third, hop].astype(F32)
        sums1[third] = total.astype(BF16)
        a0, b0 = mine[third]
        for off in (5, 15, 4, 1, 12, 3, 13, 7, 10, 8, 2, 6, 9, 14, 11):
            a, b = (a0 + off // 4) % 4, (b0 + off % 4) % 4
            pltpu.make_async_remote_copy(
                src_ref=sums1.at[third, a, b],
                dst_ref=got2.at[third, off - 1],
                send_sem=rs_send.at[4, third],
                recv_sem=rs_got.at[4, third],
                device_id=(plane(third, a, b),),
                device_id_type=MESH,
            ).start()

    for third in range(3):
        pltpu.make_async_copy(got2.at[third], got2.at[third], rs_got.at[4, third]).wait()
        a0, b0 = mine[third]
        total = sums1[third, a0, b0].astype(F32)
        total = total + jnp.sum(got2[third].astype(F32), axis=0)
        upper, lower = total[0:8], total[8:16]
        if third == 0:
            gwo[...] = upper
        else:
            gwh[:, 256 * (third - 1) : 256 * third] = upper
        if third == 2:
            gwi[...] = lower
        else:
            gwh[:, 512 + 256 * third : 768 + 256 * third] = lower

    def sent(k, size):
        sample = send.at[k, pl.ds(0, 127), :, 0:size]
        pltpu.make_async_copy(sample, sample, send_sem.at[k]).wait()

    def all_sent(k, carry):
        sent(k, CHUNK)
        return carry

    lax.fori_loop(0, LAST, all_sent, 0)
    sent(LAST, rest)
    pose_copy.wait_send()
    grad_copy.wait_send()
    for _, copy in copies1:
        copy.wait_send()
    for third in range(3):
        pltpu.make_async_copy(got2.at[third], got2.at[third], rs_send.at[4, third]).wait()


def deliver(head, gb, gwo, gwh, gwi, gb_h, gwo_h, gwh_h, gwi_h, sem):
    width = gb_h.shape[2]
    step = gb.shape[0] // BLOCKS
    copies = [
        pltpu.make_async_copy(gwo, gwo_h, sem.at[BLOCKS]),
        pltpu.make_async_copy(gwh, gwh_h, sem.at[BLOCKS + 1]),
        pltpu.make_async_copy(gwi, gwi_h, sem.at[BLOCKS + 2]),
    ]
    for block in range(BLOCKS):
        here = slice(block * step, block * step + step)
        copies.append(
            pltpu.make_async_copy(
                gb.at[here, head : head + width], gb_h.at[0, here], sem.at[block]
            )
        )
    for copy in copies:
        copy.start()
    for copy in copies:
        copy.wait()


def on_device(pose_input, w_in, w_hid, w_out, targets, basis, owner, frame_subject):
    frames, p_size = pose_input.shape
    hidden = w_hid.shape[0]
    vmem = pl.BlockSpec(memory_space=pltpu.VMEM)
    hbm = pl.BlockSpec(memory_space=pl.ANY)
    padded = CHUNKS * CHUNK
    kept = pl.pallas_call(
        kernel,
        out_shape=(
            pltpu.VMEM((p_size, padded), BF16),
            pltpu.VMEM((8, p_size), F32),
            pltpu.VMEM((8, hidden), F32),
            pltpu.VMEM((8, p_size), F32),
        ),
        in_specs=[hbm] * 8,
        out_specs=(vmem, vmem, vmem, vmem),
        scratch_shapes=[
            pltpu.VMEM(w_in.shape, BF16),
            pltpu.VMEM(w_hid.shape, BF16),
            pltpu.VMEM(w_out.shape, BF16),
            pltpu.VMEM((1, frames), jnp.int32),
            pltpu.VMEM((1, owner.shape[0]), jnp.int32),
            pltpu.VMEM((frames, padded), BF16),
            pltpu.VMEM((p_size, padded), BF16),
            pltpu.VMEM((CHUNKS, 128, 2, CHUNK), BF16),
            pltpu.VMEM((CHUNKS, 128, 2, CHUNK), BF16),
            pltpu.VMEM((256, frames), BF16),
            pltpu.VMEM((256, p_size), BF16),
            pltpu.VMEM((p_size, 256), BF16),
            pltpu.VMEM((512, p_size), BF16),
            pltpu.VMEM((hidden // 2, hidden), BF16),
            pltpu.VMEM((hidden // 2, p_size), BF16),
            pltpu.VMEM((hidden // 2, hidden), BF16),
            pltpu.VMEM((hidden // 2, 512), BF16),
            pltpu.VMEM((hidden // 2, 512), BF16),
            pltpu.VMEM((hidden // 2, 512), F32),
            pltpu.VMEM((512, hidden), F32),
            pltpu.VMEM((256, p_size), F32),
            pltpu.VMEM((512, p_size), BF16),
            pltpu.VMEM((512, hidden), BF16),
            pltpu.VMEM((hidden // 2, 256), BF16),
            pltpu.VMEM((6, hidden // 2, 256), F32),
            pltpu.VMEM((3, 4, 4, 4, 16, 256), BF16),
            pltpu.VMEM((3, 4, 4, 16, 256), BF16),
            pltpu.VMEM((3, 3, 4, 4, 16, 256), BF16),
            pltpu.VMEM((3, 15, 16, 256), BF16),
            pltpu.SemaphoreType.DMA((9,)),
            pltpu.SemaphoreType.DMA((CHUNKS,)),
            pltpu.SemaphoreType.DMA((CHUNKS,)),
            pltpu.SemaphoreType.DMA((5, 3)),
            pltpu.SemaphoreType.DMA((5, 3)),
            pltpu.SemaphoreType.REGULAR,
        ],
        compiler_params=pltpu.CompilerParams(
            collective_id=0, has_side_effects=True, vmem_limit_bytes=VMEM_LIMIT
        ),
    )(
        pose_input, targets, basis, w_in, w_hid, w_out,
        frame_subject.astype(jnp.int32).reshape(1, -1), owner.astype(jnp.int32).reshape(1, -1),
    )
    grad_basis, gwo, gwh, gwi = pl.pallas_call(
        functools.partial(deliver, p_size),
        out_shape=(
            jax.ShapeDtypeStruct(basis.shape, BF16),
            jax.ShapeDtypeStruct((8, p_size), F32),
            jax.ShapeDtypeStruct((8, hidden), F32),
            jax.ShapeDtypeStruct((8, p_size), F32),
        ),
        in_specs=[hbm] * 4,
        out_specs=(hbm,) * 4,
        scratch_shapes=[pltpu.SemaphoreType.DMA((BLOCKS + 3,))],
        compiler_params=pltpu.CompilerParams(vmem_limit_bytes=2**20),
    )(*(pltpu.with_memory_space_constraint(value, pltpu.VMEM) for value in kept))
    return gwi.T, gwh, gwo, grad_basis


def solution(mesh):
    in_specs = (
        P("dev", None),
        P(),
        P(),
        P(),
        P("dev", None),
        P("dev", None, None),
        P(),
        P("dev", None),
    )
    out_specs = (P(None, "dev"), P("dev", None), P("dev", None), P("dev", None, None))
    return jax.shard_map(
        on_device, mesh=mesh, in_specs=in_specs, out_specs=out_specs, check_vma=False
    )
```

```python
import functools
import jax
import jax.numpy as jnp
from jax import lax
from jax.experimental import pallas as pl
from jax.experimental.pallas import tpu as pltpu
from jax.sharding import PartitionSpec as P

MESH = pl.DeviceIdType.MESH
F32, BF16 = jnp.float32, jnp.bfloat16
CHUNKS, CHUNK, PIECE = 7, 2304, 768
STRIDE = 37
LAST = CHUNKS - 1
VMEM_LIMIT = 54 * 2**20
BLOCKS = 4


def mm(left, right):
    return jnp.dot(left, right, preferred_element_type=F32)


def mm_t(left, right):
    return lax.dot_general(left, right, (((1,), (1,)), ((), ())), preferred_element_type=F32)


def silu_slope(value, sig):
    return sig * (1.0 + value * (1.0 - sig))


def device(z, y, x, c):
    return ((z * 4 + y) * 4 + x) * 2 + c


def peer(me, step):
    return lax.rem(me + step * STRIDE, 128)


def select_matrix(subject, owner):
    n = owner.shape[1]
    down = lax.broadcasted_iota(jnp.int32, (n, n), 0)
    across = lax.broadcasted_iota(jnp.int32, (n, n), 1)
    subject_row = subject.astype(F32)
    wide = jnp.broadcast_to(subject_row, (n, n))
    subject_col = jnp.sum(jnp.where(down == across, wide, 0.0), axis=1, keepdims=True)
    same = subject_col == subject_row
    rank = jnp.sum(jnp.where(same & (down < across), 1.0, 0.0), axis=0, keepdims=True)
    owner = jnp.broadcast_to(owner.astype(F32), (n, n))
    owner_col = jnp.sum(jnp.where(down == across, owner, 0.0), axis=1, keepdims=True)
    named = subject_row == down.astype(F32)
    slot = jnp.sum(jnp.where(named, owner_col, 0.0), axis=0, keepdims=True)
    row = 2.0 * slot + rank
    rows = lax.broadcasted_iota(jnp.int32, (2 * n, n), 0).astype(F32)
    return jnp.where(rows == row, 1.0, 0.0).astype(BF16)


def half_matrix(c, rows, columns):
    row = lax.broadcasted_iota(jnp.int32, (rows, columns), 0)
    column = lax.broadcasted_iota(jnp.int32, (rows, columns), 1)
    return jnp.where(column == 2 * row - row % 8 + 8 * c, 1.0, 0.0).astype(BF16)


def kernel(
    pose_h, tgt_h, basis_h, w_in_h, w_hid_h, w_out_h, subject_h, owner_h,
    gb, gwo, gwh, gwi,
    w_in, w_hid, w_out, subject, owner, rows, basis, send, got, pick, feat, feat_t, pose, half, w_in_t, w_hid_half,
    h1_t, h2_t, slope1_t, slope2, grad_feat, grad, back_two, back_one_t,
    halves, sums0, sums1, got1, got2,
    load_sem, send_sem, got_sem, rs_send, rs_got, vouched,
):
    me = lax.axis_index("dev")
    z, y, x, c = me // 32, (me // 8) % 4, (me // 2) % 4, me % 2
    width = tgt_h.shape[1]
    scale = width ** (-0.5)
    head = pose_h.shape[1]
    first = CHUNK - head
    rest = head + width - LAST * CHUNK

    pairs = [
        (subject_h, subject),
        (owner_h, owner),
        (pose_h, rows.at[:, 0:head]),
        (tgt_h.at[:, 0:first], rows.at[:, head:CHUNK]),
        (tgt_h.at[:, first:width], rows.at[:, CHUNK : head + width]),
        (w_in_h, w_in),
        (w_hid_h, w_hid),
        (w_out_h, w_out),
        (basis_h.at[0], basis.at[:, head : head + width]),
    ]
    loads = [
        pltpu.make_async_copy(src, dst, load_sem.at[at]) for at, (src, dst) in enumerate(pairs)
    ]
    for load in loads[:4]:
        load.start()

    barrier = pltpu.get_barrier_semaphore()

    line, block_of = me % 8, me // 8

    def mate(step):
        return block_of * 8 + lax.rem(line + step, 8)

    def across(step):
        return lax.rem(block_of + step, 16) * 8 + line

    def greet_across(step, carry):
        pl.semaphore_signal(barrier, inc=1, device_id=(across(step),), device_id_type=MESH)
        return carry

    def greet_mate(step, carry):
        pl.semaphore_signal(barrier, inc=1, device_id=(mate(step),), device_id_type=MESH)
        return carry

    def vouch(step, carry):
        pl.semaphore_signal(vouched, inc=1, device_id=(mate(step),), device_id_type=MESH)
        return carry

    lax.fori_loop(1, 16, greet_across, 0)
    lax.fori_loop(1, 8, greet_mate, 0)
    loads[0].wait()
    loads[1].wait()
    pick[...] = select_matrix(subject[...], owner[...])

    def fill(k):
        def piece(j, carry):
            at = pl.multiple_of(k * CHUNK + j * PIECE, 128)
            to = pl.multiple_of(j * PIECE, 128)
            block = mm(pick[...], rows[:, pl.ds(at, PIECE)]).astype(BF16)
            send[k, :, :, pl.ds(to, PIECE)] = block.reshape(128, 2, PIECE)
            return carry

        lax.fori_loop(0, CHUNK // PIECE, piece, 0)

    def ship_to(k, size, to):
        pltpu.make_async_remote_copy(
            src_ref=send.at[k, to, :, 0:size],
            dst_ref=got.at[k, me, :, 0:size],
            send_sem=send_sem.at[k],
            recv_sem=got_sem.at[k],
            device_id=(to,),
            device_id_type=MESH,
        ).start()

    def keep(k, size):
        pltpu.make_async_copy(
            send.at[k, me, :, 0:size], got.at[k, me, :, 0:size], got_sem.at[k]
        ).start()

    def ship(k, size):
        keep(k, size)

        def one(step, carry):
            ship_to(k, size, peer(me, step))
            return carry

        lax.fori_loop(1, 128, one, 0)

    def first_across(step, carry):
        ship_to(0, CHUNK, across(lax.rem(step * 4, 15) + 1))
        return carry

    def first_mate(step, carry):
        ship_to(0, CHUNK, mate(step))
        return carry

    def first_others(step, carry):
        to = lax.rem(block_of + 1 + lax.rem(step, 15), 16) * 8
        ship_to(0, CHUNK, to + lax.rem(line + 1 + lax.rem(step, 7), 8))
        return carry

    loads[2].wait()
    loads[3].wait()
    loads[4].start()
    fill(0)
    pl.semaphore_wait(barrier, 22)
    lax.fori_loop(1, 8, vouch, 0)
    keep(0, CHUNK)
    lax.fori_loop(0, 15, first_across, 0)
    lax.fori_loop(1, 8, first_mate, 0)
    pl.semaphore_wait(vouched, 7)
    lax.fori_loop(0, 105, first_others, 0)
    for load in loads[5:]:
        load.start()
    rows[:, head + width :] = jnp.zeros((rows.shape[0], rows.shape[1] - head - width), BF16)
    basis[:, head + width :] = jnp.zeros((basis.shape[0], basis.shape[1] - head - width), BF16)
    basis[:, 0:head] = jnp.zeros((basis.shape[0], head), BF16)
    got[LAST, :, :, rest:] = jnp.zeros((128, 2, CHUNK - rest), BF16)
    loads[4].wait()

    def more(k, carry):
        fill(k)
        ship(k, CHUNK)
        return carry

    lax.fori_loop(1, LAST, more, 0)
    fill(LAST)
    ship(LAST, rest)

    for load in loads[5:]:
        load.wait()
    half[...] = half_matrix(c, half.shape[0], half.shape[1])
    w_in_t[...] = mm_t(half[...], w_in[...]).astype(BF16)
    w_hid_half[...] = mm(half[...], w_hid[...]).astype(BF16)

    def arrived(k, size):
        block = got.at[k, :, :, 0:size]
        pltpu.make_async_copy(block, block, got_sem.at[k]).wait()

    def forward(part):
        at = 256 * part
        pre_one = mm(pose[at : at + 256, :], w_in[...])
        hidden_one = (pre_one * jax.nn.sigmoid(pre_one)).astype(BF16)
        pre_two = mm(hidden_one, w_hid[...])
        sig_two = jax.nn.sigmoid(pre_two)
        hidden_two = (pre_two * sig_two).astype(BF16)
        slope2[at : at + 256, :] = silu_slope(pre_two, sig_two)
        h2_t[:, at : at + 256] = mm_t(half[...], hidden_two).astype(BF16)
        return hidden_two

    twin = device(z, y, x, 1 - c)

    def to_twin(ref, slot):
        return pltpu.make_async_remote_copy(
            src_ref=ref.at[0:256],
            dst_ref=ref.at[256:512],
            send_sem=rs_send.at[0, slot],
            recv_sem=rs_got.at[0, slot],
            device_id=(twin,),
            device_id_type=MESH,
        )

    arrived(0, CHUNK)
    pose[0:256, :] = got[0, :, :, 0:head].reshape(256, head)
    pose_copy = to_twin(pose, 0)
    pose_copy.start()
    feat[...] = mm(forward(0), w_out[...]).astype(BF16)
    feat_t[...] = feat[...].T
    grad_feat[...] = jnp.zeros_like(grad_feat)

    def correct(k, unroll=False):
        def piece(j, carry):
            at = pl.multiple_of(k * CHUNK + j * PIECE, 128)
            to = pl.multiple_of(j * PIECE, 128)
            slab = basis[:, pl.ds(at, PIECE)]
            target = got[k, :, :, pl.ds(to, PIECE)].reshape(256, PIECE)
            corr = ((mm(feat[...], slab) - target.astype(F32)) * scale).astype(BF16)
            gb[:, pl.ds(at, PIECE)] = corr
            grad_feat[...] += mm_t(corr, slab)
            return carry

        lax.fori_loop(0, CHUNK // PIECE, piece, 0, unroll=unroll)

    def outer(k):
        def piece(j, carry):
            at = pl.multiple_of(k * CHUNK + j * PIECE, 128)
            gb[:, pl.ds(at, PIECE)] = mm(feat_t[...], gb[:, pl.ds(at, PIECE)]).astype(BF16)
            return carry

        lax.fori_loop(0, CHUNK // PIECE, piece, 0)

    def turn(k, carry):
        arrived(k, CHUNK)
        correct(k)
        outer(k)
        return carry

    correct(0)
    outer(0)
    lax.fori_loop(1, 3, turn, 0)
    pose_copy.wait_recv()
    forward(1)
    pre_t = mm_t(w_in_t[...], pose[...])
    sig_t = jax.nn.sigmoid(pre_t)
    h1_t[...] = (pre_t * sig_t).astype(BF16)
    slope1_t[...] = silu_slope(pre_t, sig_t)
    lax.fori_loop(3, LAST, turn, 0)
    arrived(LAST, rest)
    correct(LAST, unroll=True)

    grad[0:256, :] = grad_feat[...].astype(BF16)
    grad_copy = to_twin(grad, 1)
    grad_copy.start()

    def backward(part):
        at = 256 * part
        back = mm_t(grad[at : at + 256, :], w_out[...]) * slope2[at : at + 256, :]
        back_two[at : at + 256, :] = back.astype(BF16)

    def product(third, lower, part):
        at = slice(256 * part, 256 * part + 256)
        if (third, lower) == (0, False):
            return mm(h2_t[:, at], grad[at, :])
        if (third, lower) == (2, True):
            back = mm_t(w_hid_half[...], back_two[at, :]) * slope1_t[:, at]
            back_one_t[...] = back.astype(BF16)
            return mm(back_one_t[...], pose[at, :])
        first_column = 256 * (third - 1) + (768 if lower else 0)
        return mm(h1_t[:, at], back_two[at, first_column : first_column + 256])

    backward(0)
    for third in range(3):
        for lower in (False, True):
            halves[2 * third + lower] = product(third, lower, 0)
    grad_copy.wait_recv()
    backward(1)

    spots = (x, y, z)

    def along(third, value):
        zyx = [z, y, x]
        zyx[2 - third] = value
        return device(*zyx, c)

    def rows1(ref, third, value):
        view = ref.at[third]
        if third == 0:
            return view.at[:, :, value]
        if third == 1:
            return view.at[:, value]
        return view.at[value]

    copies1 = []
    for third in range(3):
        upper = halves[2 * third] + product(third, False, 1)
        lower = halves[2 * third + 1] + product(third, True, 1)
        both = jnp.concatenate([upper.reshape(64, 8, 256), lower.reshape(64, 8, 256)], axis=1)
        sums0[third] = both.astype(BF16).reshape(4, 4, 4, 16, 256)
        for hop in (2, 1, 3):
            value = (spots[third] + hop) % 4
            copy = pltpu.make_async_remote_copy(
                src_ref=rows1(sums0, third, value),
                dst_ref=got1.at[third, hop - 1],
                send_sem=rs_send.at[hop, third],
                recv_sem=rs_got.at[hop, third],
                device_id=(along(third, value),),
                device_id_type=MESH,
            )
            copy.start()
            copies1.append((third, copy))
    outer(LAST)

    def plane(third, a, b):
        if third == 0:
            return device(a, b, x, c)
        if third == 1:
            return device(a, y, b, c)
        return device(z, a, b, c)

    mine = ((z, y), (z, x), (y, x))
    for third in range(3):
        for which, copy in copies1:
            if which == third:
                copy.wait_recv()
        if third == 0:
            own = sums0[third, :, :, x]
        elif third == 1:
            own = sums0[third, :, y]
        else:
            own = sums0[third, z]
        total = own.astype(F32)
        for hop in range(3):
            total = total + got1[third, hop].astype(F32)
        sums1[third] = total.astype(BF16)
        a0, b0 = mine[third]
        for off in (5, 15, 4, 1, 12, 3, 13, 7, 10, 8, 2, 6, 9, 14, 11):
            a, b = (a0 + off // 4) % 4, (b0 + off % 4) % 4
            pltpu.make_async_remote_copy(
                src_ref=sums1.at[third, a, b],
                dst_ref=got2.at[third, off - 1],
                send_sem=rs_send.at[4, third],
                recv_sem=rs_got.at[4, third],
                device_id=(plane(third, a, b),),
                device_id_type=MESH,
            ).start()

    for third in range(3):
        pltpu.make_async_copy(got2.at[third], got2.at[third], rs_got.at[4, third]).wait()
        a0, b0 = mine[third]
        total = sums1[third, a0, b0].astype(F32)
        total = total + jnp.sum(got2[third].astype(F32), axis=0)
        upper, lower = total[0:8], total[8:16]
        if third == 0:
            gwo[...] = upper
        else:
            gwh[:, 256 * (third - 1) : 256 * third] = upper
        if third == 2:
            gwi[...] = lower
        else:
            gwh[:, 512 + 256 * third : 768 + 256 * third] = lower

    def sent(k, size):
        sample = send.at[k, pl.ds(0, 127), :, 0:size]
        pltpu.make_async_copy(sample, sample, send_sem.at[k]).wait()

    def all_sent(k, carry):
        sent(k, CHUNK)
        return carry

    lax.fori_loop(0, LAST, all_sent, 0)
    sent(LAST, rest)
    pose_copy.wait_send()
    grad_copy.wait_send()
    for _, copy in copies1:
        copy.wait_send()
    for third in range(3):
        pltpu.make_async_copy(got2.at[third], got2.at[third], rs_send.at[4, third]).wait()


def deliver(head, gb, gwo, gwh, gwi, gb_h, gwo_h, gwh_h, gwi_h, sem):
    width = gb_h.shape[2]
    step = gb.shape[0] // BLOCKS
    copies = [
        pltpu.make_async_copy(gwo, gwo_h, sem.at[BLOCKS]),
        pltpu.make_async_copy(gwh, gwh_h, sem.at[BLOCKS + 1]),
        pltpu.make_async_copy(gwi, gwi_h, sem.at[BLOCKS + 2]),
    ]
    for block in range(BLOCKS):
        here = slice(block * step, block * step + step)
        copies.append(
            pltpu.make_async_copy(
                gb.at[here, head : head + width], gb_h.at[0, here], sem.at[block]
            )
        )
    for copy in copies:
        copy.start()
    for copy in copies:
        copy.wait()


def on_device(pose_input, w_in, w_hid, w_out, targets, basis, owner, frame_subject):
    frames, p_size = pose_input.shape
    hidden = w_hid.shape[0]
    vmem = pl.BlockSpec(memory_space=pltpu.VMEM)
    hbm = pl.BlockSpec(memory_space=pl.ANY)
    padded = CHUNKS * CHUNK
    kept = pl.pallas_call(
        kernel,
        out_shape=(
            pltpu.VMEM((p_size, padded), BF16),
            pltpu.VMEM((8, p_size), F32),
            pltpu.VMEM((8, hidden), F32),
            pltpu.VMEM((8, p_size), F32),
        ),
        in_specs=[hbm] * 8,
        out_specs=(vmem, vmem, vmem, vmem),
        scratch_shapes=[
            pltpu.VMEM(w_in.shape, BF16),
            pltpu.VMEM(w_hid.shape, BF16),
            pltpu.VMEM(w_out.shape, BF16),
            pltpu.VMEM((1, frames), jnp.int32),
            pltpu.VMEM((1, owner.shape[0]), jnp.int32),
            pltpu.VMEM((frames, padded), BF16),
            pltpu.VMEM((p_size, padded), BF16),
            pltpu.VMEM((CHUNKS, 128, 2, CHUNK), BF16),
            pltpu.VMEM((CHUNKS, 128, 2, CHUNK), BF16),
            pltpu.VMEM((256, frames), BF16),
            pltpu.VMEM((256, p_size), BF16),
            pltpu.VMEM((p_size, 256), BF16),
            pltpu.VMEM((512, p_size), BF16),
            pltpu.VMEM((hidden // 2, hidden), BF16),
            pltpu.VMEM((hidden // 2, p_size), BF16),
            pltpu.VMEM((hidden // 2, hidden), BF16),
            pltpu.VMEM((hidden // 2, 512), BF16),
            pltpu.VMEM((hidden // 2, 512), BF16),
            pltpu.VMEM((hidden // 2, 512), F32),
            pltpu.VMEM((512, hidden), F32),
            pltpu.VMEM((256, p_size), F32),
            pltpu.VMEM((512, p_size), BF16),
            pltpu.VMEM((512, hidden), BF16),
            pltpu.VMEM((hidden // 2, 256), BF16),
            pltpu.VMEM((6, hidden // 2, 256), F32),
            pltpu.VMEM((3, 4, 4, 4, 16, 256), BF16),
            pltpu.VMEM((3, 4, 4, 16, 256), BF16),
            pltpu.VMEM((3, 3, 4, 4, 16, 256), BF16),
            pltpu.VMEM((3, 15, 16, 256), BF16),
            pltpu.SemaphoreType.DMA((9,)),
            pltpu.SemaphoreType.DMA((CHUNKS,)),
            pltpu.SemaphoreType.DMA((CHUNKS,)),
            pltpu.SemaphoreType.DMA((5, 3)),
            pltpu.SemaphoreType.DMA((5, 3)),
            pltpu.SemaphoreType.REGULAR,
        ],
        compiler_params=pltpu.CompilerParams(
            collective_id=0, has_side_effects=True, vmem_limit_bytes=VMEM_LIMIT
        ),
    )(
        pose_input, targets, basis, w_in, w_hid, w_out,
        frame_subject.astype(jnp.int32).reshape(1, -1), owner.astype(jnp.int32).reshape(1, -1),
    )
    grad_basis, gwo, gwh, gwi = pl.pallas_call(
        functools.partial(deliver, p_size),
        out_shape=(
            jax.ShapeDtypeStruct(basis.shape, BF16),
            jax.ShapeDtypeStruct((8, p_size), F32),
            jax.ShapeDtypeStruct((8, hidden), F32),
            jax.ShapeDtypeStruct((8, p_size), F32),
        ),
        in_specs=[hbm] * 4,
        out_specs=(hbm,) * 4,
        scratch_shapes=[pltpu.SemaphoreType.DMA((BLOCKS + 3,))],
        compiler_params=pltpu.CompilerParams(vmem_limit_bytes=2**20),
    )(*(pltpu.with_memory_space_constraint(value, pltpu.VMEM) for value in kept))
    return gwi.T, gwh, gwo, grad_basis


def solution(mesh):
    in_specs = (
        P("dev", None),
        P(),
        P(),
        P(),
        P("dev", None),
        P("dev", None, None),
        P(),
        P("dev", None),
    )
    out_specs = (P(None, "dev"), P("dev", None), P("dev", None), P("dev", None, None))
    return jax.shard_map(
        on_device, mesh=mesh, in_specs=in_specs, out_specs=out_specs, check_vma=False
    )
```
